512 devices in a mesh: dp: 8 (over z_hi, x), ctx: 16 (over y, core), nbr: 4 (over z_lo).
Axes of the slice: x: 4, y: 8, z: 8 (z_hi: 2, z_lo: 4; z = z_hi * 4 + z_lo), core: 2. Of those that a mesh axis runs over, the one named last changes fastest.
Arguments:
- queries: bfloat16 [8, 4096, 2048], P('dp', 'ctx', 'nbr'), may hold values from -140 to 140
- cotangent: bfloat16 [8, 4096, 2048], P('dp', 'ctx', 'nbr'), may hold values from -6 to 6
- encoded: bfloat16 [8, 256, 64, 896], P('dp', 'ctx', 'nbr'), may hold values from -6 to 6
- kv_weight: bfloat16 [2, 896, 2048], P(None, None, 'nbr'), may hold values from -0.1875 to 0.1875
- neighbour_ids: int32 [8, 64, 4], P('dp', 'ctx'), may hold values from 0 to 255, as said below
Outputs:
- attended: bfloat16 [8, 4096, 2048], P('dp', 'ctx', 'nbr')
- query_grad: bfloat16 [8, 4096, 2048], P('dp', 'ctx', 'nbr')
- encoded_grad: bfloat16 [8, 256, 64, 896], P('dp', 'ctx', 'nbr')
- weight_grad: float32 [2, 896, 2048], P(None, 'dp', 'nbr')
The draws below stay inside these ranges and needn't reach their ends.
Inputs may be any that keep to these rules, and one draw needn't show every extreme that they name: `neighbour_ids`: for every batch and every d < 16, the ids of the spans d * 4 to (d + 1) * 4 - 1 are exactly the blocks s * 16 + d + j for all s < 16 and j < 1, each named once.
All inputs are finite; a program needn't handle non-finite values.
Results may differ from the reference program's by a relative error of at most 0.029.
The reference program's roundings to bfloat16 on the way count: a program that leaves them out, or rounds other values in their place, can miss the bound.
Values may be sent and summed in bfloat16 or wider, within the bound.
No kernel may reach another device: no remote copies, remote signals or barrier semaphores. Data moves between devices by JAX's collectives and lax.ppermute only.
A program may use at most 128 MiB of HBM per device.

```python
import math
import jax
import jax.numpy as jnp
from jax import lax

HEADS = 16
HEAD_DIM = 128
ENC = 896
SPAN = 64
PART = 64
SPAN_DEV = 4
UNIT_DEV = 16
GROUP = 1
GROUPS = 4
SEQ = 4096
UNITS = 256
BATCH = 8


def draw_queries(key, part):
    key = jax.random.fold_in(key, 11)
    base = jnp.clip(jax.random.normal(key, (BATCH, SEQ, HEADS * HEAD_DIM), jnp.float32), -4.5, 4.5)
    return base.astype(jnp.bfloat16)


def draw_neighbour_ids(key, part):
    key = jax.random.fold_in(key, 7)
    owners_count = UNITS // UNIT_DEV
    key_list = jax.random.split(key, BATCH * owners_count)
    orders = jax.vmap(lambda single: jax.random.permutation(single, UNIT_DEV))(key_list)
    owner_rows = (jnp.arange(BATCH * owners_count, dtype=jnp.int32) % owners_count)[:, None]
    source_rows = orders // GROUP
    slot_rows = owner_rows * GROUP + orders % GROUP
    id_values = source_rows * UNIT_DEV + slot_rows
    return id_values.reshape(BATCH, owners_count * SPAN_DEV, 4).astype(jnp.int32)


def block_levels(rng, shape, cuts, smallest, largest):
    factor_of, own = 1.0, jax.random.fold_in(rng, 6)
    for position, parts in cuts:
        heights = jnp.exp(jax.random.uniform(jax.random.fold_in(own, position), (parts,), jnp.float32, smallest / len(cuts), largest / len(cuts)))
        factor_of = factor_of * jnp.repeat(heights, shape[position] // parts).reshape([-1 if axis == position else 1 for axis in range(len(shape))])
    return factor_of


def gaussian(rng, shape, scale, bound, cuts=(), kind=jnp.bfloat16):
    result = scale * jax.random.normal(rng, shape, jnp.float32)
    if cuts:
        result = result * block_levels(rng, shape, cuts, -0.22, 0.18)
    return jnp.clip(result, -bound, bound).astype(kind)


def setup_inputs(seed: int = 0) -> dict:
    seeds = jax.random.split(jax.random.key(seed), 6)
    queries = draw_queries(jax.random.fold_in(seeds[5], 71), 0)
    cotangent = gaussian(seeds[1], (BATCH, SEQ, HEADS * HEAD_DIM), 1.0, 6.0, ((0, 8), (1, 16), (2, 4)))
    encoded = gaussian(seeds[2], (BATCH, UNITS, PART, ENC), 1.0, 6.0, ((0, 8), (1, 16), (2, 4)))
    kv_weight = gaussian(seeds[3], (2, ENC, HEADS * HEAD_DIM), ENC ** -0.5, 0.1875, ((2, 4),))
    neighbour_ids = draw_neighbour_ids(jax.random.fold_in(seeds[5], 71), 0)
    return {"queries": queries, "cotangent": cotangent, "encoded": encoded, "kv_weight": kv_weight, "neighbour_ids": neighbour_ids}


def rounded(values):
    return lax.optimization_barrier(values.astype(jnp.bfloat16)).astype(jnp.float32)

def attend_forward(query_blocks, span_keys, span_values):
    block_count, row_count, row_width = query_blocks.shape
    head_count = row_width // HEAD_DIM
    key_count = span_keys.shape[1]
    scale_factor = 1.0 / math.sqrt(HEAD_DIM)
    query_heads = query_blocks.reshape(block_count, row_count, head_count, HEAD_DIM)
    key_heads = span_keys.reshape(block_count, key_count, head_count, HEAD_DIM)
    value_heads = span_values.reshape(block_count, key_count, head_count, HEAD_DIM)
    scores = jnp.einsum('cqhd,ckhd->chqk', query_heads, key_heads) * scale_factor
    score_top = lax.optimization_barrier(jnp.max(scores, axis=-1, keepdims=True))
    raised = jnp.exp(scores - score_top)
    weights = raised / lax.optimization_barrier(jnp.sum(raised, axis=-1, keepdims=True))
    weights_low = rounded(weights)
    mixed = jnp.einsum('chqk,ckhd->cqhd', weights_low, value_heads)
    attended = rounded(mixed).reshape(block_count, row_count, row_width)
    return (attended, (query_heads, key_heads, value_heads, weights, weights_low))

def attend_backward(saved, grad_blocks):
    query_heads, key_heads, value_heads, weights, weights_low = saved
    block_count, row_count, head_count, head_dim = query_heads.shape
    key_count = key_heads.shape[1]
    scale_factor = 1.0 / math.sqrt(HEAD_DIM)
    grad_heads = grad_blocks.reshape(block_count, row_count, head_count, head_dim)
    value_grads = jnp.einsum('chqk,cqhd->ckhd', weights_low, grad_heads)
    weight_grads = jnp.einsum('cqhd,ckhd->chqk', grad_heads, value_heads)
    inner = lax.optimization_barrier(jnp.sum(weights * weight_grads, axis=-1, keepdims=True))
    score_grads = rounded(weights * (weight_grads - inner) * scale_factor)
    query_grads = rounded(jnp.einsum('chqk,ckhd->cqhd', score_grads, key_heads))
    key_grads = jnp.einsum('chqk,cqhd->ckhd', score_grads, query_heads)
    row_width = head_count * head_dim
    return (query_grads.reshape(block_count, row_count, row_width), key_grads.reshape(block_count, key_count, row_width), value_grads.reshape(block_count, key_count, row_width))

def reference(queries, cotangent, encoded, kv_weight, neighbour_ids):
    batch_count, seq_len, row_width = queries.shape
    block_count = seq_len // SPAN
    lead_rows = SPAN - 1
    group_width = row_width // GROUPS
    key_weight = kv_weight[0].astype(jnp.float32)
    value_weight = kv_weight[1].astype(jnp.float32)
    weight_grad = jnp.zeros((2, ENC, row_width), jnp.float32)
    attended_list = []
    query_grad_list = []
    encoded_grad_list = []
    padding = jnp.zeros((lead_rows, row_width), jnp.float32)
    for batch_index in range(batch_count):
        encoded_rows = encoded[batch_index].astype(jnp.float32)
        key_rows = rounded(jnp.einsum('upe,ef->upf', encoded_rows, key_weight))
        value_rows = rounded(jnp.einsum('upe,ef->upf', encoded_rows, value_weight))
        id_flat = neighbour_ids[batch_index].reshape(-1).astype(jnp.int32)
        span_keys = jnp.take(key_rows, id_flat, axis=0).reshape(block_count, 4 * PART, row_width)
        span_values = jnp.take(value_rows, id_flat, axis=0).reshape(block_count, 4 * PART, row_width)
        query_rows = jnp.concatenate((queries[batch_index, lead_rows:].astype(jnp.float32), padding), axis=0)
        grad_rows = jnp.concatenate((cotangent[batch_index, lead_rows:].astype(jnp.float32), padding), axis=0)
        query_rows = query_rows.reshape(block_count, SPAN, row_width)
        grad_rows = grad_rows.reshape(block_count, SPAN, row_width)
        attended_blocks, saved = attend_forward(query_rows, span_keys, span_values)
        query_grad_blocks, key_grads, value_grads = attend_backward(saved, grad_rows)
        attended = jnp.concatenate((padding, attended_blocks.reshape(seq_len, row_width)[:seq_len - lead_rows]), axis=0)
        query_grad = jnp.concatenate((padding, query_grad_blocks.reshape(seq_len, row_width)[:seq_len - lead_rows]), axis=0)
        attended_list.append(attended)
        query_grad_list.append(query_grad)
        key_low = rounded(key_grads).reshape(block_count * 4, PART, row_width)
        value_low = rounded(value_grads).reshape(block_count * 4, PART, row_width)
        unit_keys = jnp.zeros((UNITS, PART, row_width), jnp.float32).at[id_flat].add(key_low)
        unit_values = jnp.zeros((UNITS, PART, row_width), jnp.float32).at[id_flat].add(value_low)
        weight_grad = weight_grad + jnp.stack((jnp.einsum('upe,upf->ef', encoded_rows, unit_keys), jnp.einsum('upe,upf->ef', encoded_rows, unit_values)), axis=0)
        encoded_grad = jnp.zeros((UNITS, PART, ENC), jnp.float32)
        for group_index in range(GROUPS):
            first = group_index * group_width
            last = first + group_width
            partial_term = jnp.einsum('upf,ef->upe', unit_keys[:, :, first:last], key_weight[:, first:last])
            partial_term = partial_term + jnp.einsum('upf,ef->upe', unit_values[:, :, first:last], value_weight[:, first:last])
            encoded_grad = encoded_grad + rounded(partial_term)
        encoded_grad_list.append(encoded_grad)
    attended_all = jnp.stack(attended_list, axis=0).astype(jnp.bfloat16)
    query_grad_all = jnp.stack(query_grad_list, axis=0).astype(jnp.bfloat16)
    encoded_grad_all = jnp.stack(encoded_grad_list, axis=0).astype(jnp.bfloat16)
    return (attended_all, query_grad_all, encoded_grad_all, weight_grad)
```

```python
import math

import jax
import jax.numpy as jnp
from jax import lax
from jax.experimental import pallas as pl
from jax.experimental.pallas import tpu as pltpu
from jax.sharding import PartitionSpec as P

HEAD_DIM = 128
SPAN = 64
PART = 64
LEAD = SPAN - 1
SCALE = 1.0 / math.sqrt(HEAD_DIM)
NT = (((1,), (1,)), ((), ()))
TN = (((0,), (0,)), ((), ()))
NN = (((1,), (0,)), ((), ()))


def dot(a, b, dims):
    return lax.dot_general(a, b, dims, preferred_element_type=jnp.float32)


def attention_kernel(slots, heads, piece, units_ref, q_ref, g_ref, *refs):
    kv_refs = refs[:slots]
    att_ref, dq_ref = refs[slots : slots + 2]
    dkv_refs = refs[slots + 2 :]
    width = heads * HEAD_DIM
    spans = q_ref.shape[0] // SPAN
    for j in range(spans):
        starts = [pl.multiple_of(units_ref[j * 4 + r] * piece, piece) for r in range(4)]
        rows = pl.ds(j * SPAN, SPAN)
        for h in range(heads):
            cols = pl.ds(h * HEAD_DIM, HEAD_DIM)
            vcols = pl.ds(width + h * HEAD_DIM, HEAD_DIM)
            q = q_ref[rows, cols]
            g = g_ref[rows, cols]
            k = jnp.concatenate([ref[pl.ds(s, piece), cols] for s in starts for ref in kv_refs], axis=0)
            v = jnp.concatenate([ref[pl.ds(s, piece), vcols] for s in starts for ref in kv_refs], axis=0)
            scores = dot(q, k, NT) * SCALE
            top = jnp.max(scores, axis=-1, keepdims=True)
            raised = jnp.exp(scores - top)
            weights = raised / jnp.sum(raised, axis=-1, keepdims=True)
            low = weights.astype(jnp.bfloat16)
            d_weights = dot(g, v, NT)
            inner = jnp.sum(weights * d_weights, axis=-1, keepdims=True)
            d_scores = (weights * (d_weights - inner) * SCALE).astype(jnp.bfloat16)
            att_ref[rows, cols] = dot(low, v, NN).astype(jnp.bfloat16)
            dq_ref[rows, cols] = dot(d_scores, k, NN).astype(jnp.bfloat16)
            dk = dot(d_scores, q, TN).astype(jnp.bfloat16)
            dv = dot(low, g, TN).astype(jnp.bfloat16)
            for r, s in enumerate(starts):
                for n, ref in enumerate(dkv_refs):
                    at = (r * slots + n) * piece
                    ref[pl.ds(s, piece), cols] = dk[at : at + piece]
                    ref[pl.ds(s, piece), vcols] = dv[at : at + piece]


def attention(units, q, g, kvs, piece):
    slots = len(kvs)
    rows, width = q.shape
    heads = width // HEAD_DIM

    def body(*refs):
        attention_kernel(slots, heads, piece, *refs)

    vmem = pl.BlockSpec(memory_space=pltpu.VMEM)
    return pl.pallas_call(
        body,
        out_shape=[jax.ShapeDtypeStruct((rows, width), jnp.bfloat16)] * 2
        + [jax.ShapeDtypeStruct(kv.shape, jnp.bfloat16) for kv in kvs],
        in_specs=[pl.BlockSpec(memory_space=pltpu.SMEM)] + [vmem] * (2 + slots),
        out_specs=[vmem] * (2 + slots),
        compiler_params=pltpu.CompilerParams(vmem_limit_bytes=48 * 1024 * 1024),
        name="attention",
    )(units, q, g, *kvs)


def permute(x, axis, to):
    n = lax.axis_size(axis)
    return lax.ppermute(x, axis, [(i, to(i)) for i in range(n) if 0 <= to(i) < n])


def shards(queries, cotangent, encoded, kv_weight, neighbour_ids):
    q, g, enc = queries[0], cotangent[0], encoded[0]
    tokens, width = q.shape
    units, piece, enc_width = enc.shape
    groups = lax.axis_size("nbr")
    ctx = lax.axis_index("ctx")
    dp = lax.axis_index("dp")
    joined = jnp.concatenate((kv_weight[0], kv_weight[1]), axis=1)

    head = jnp.concatenate((q[:LEAD], g[:LEAD]), axis=1)
    ahead = permute(head, "ctx", lambda i: i - 1)
    q_rows = jnp.concatenate((q[LEAD:], ahead[:, :width]), axis=0)
    g_rows = jnp.concatenate((g[LEAD:], ahead[:, width:]), axis=0)

    own = lax.all_to_all(enc, "ctx", split_axis=0, concat_axis=0, tiled=True).reshape(units * piece, enc_width)
    slots = [own] + [permute(own, "nbr", lambda i, k=k: (i + k) % groups) for k in range(1, groups)]
    kvs = [dot(x, joined, NN).astype(jnp.bfloat16) for x in slots]

    unit_of = (neighbour_ids[0] // units).reshape(-1)
    att, dq, *dkvs = attention(unit_of, q_rows, g_rows, kvs, piece)

    partials = [dot(d, joined, NT).astype(jnp.bfloat16) for d in dkvs]
    terms = [permute(partials[k], "nbr", lambda i, k=k: (i - k) % groups) for k in range(1, groups)]
    total = partials[0].astype(jnp.float32)
    for t in terms:
        total = total + t.astype(jnp.float32)
    total = total.astype(jnp.bfloat16).reshape(units, piece, enc_width)
    encoded_grad = lax.all_to_all(total, "ctx", split_axis=0, concat_axis=0, tiled=True)

    tail = jnp.concatenate((att[tokens - LEAD :], dq[tokens - LEAD :]), axis=1)
    behind = permute(tail, "ctx", lambda i: i + 1)
    attended = jnp.concatenate((behind[:, :width], att[: tokens - LEAD]), axis=0)
    query_grad = jnp.concatenate((behind[:, width:], dq[: tokens - LEAD]), axis=0)

    x_all = jnp.concatenate(slots, axis=0)
    d_all = jnp.concatenate(dkvs, axis=0).reshape(-1, 2, width)
    core = ctx % 2
    d_mine = lax.dynamic_index_in_dim(d_all, core, 1, keepdims=False)
    d_other = lax.dynamic_index_in_dim(d_all, 1 - core, 1, keepdims=False)
    away = permute(dot(x_all, d_other, TN).astype(jnp.bfloat16), "ctx", lambda i: i ^ 1)
    part = dot(x_all, d_mine, TN) + away.astype(jnp.float32)
    rows = enc_width // 8
    part = part.reshape(2, 4, rows, width)
    low = part.astype(jnp.bfloat16)
    x = dp % 4
    held = lax.dynamic_index_in_dim(part, x, 1, keepdims=False)
    for k in (1, 3, 2):
        piece_k = lax.dynamic_index_in_dim(low, (x + k) % 4, 1, keepdims=False)
        held = held + permute(piece_k, "dp", lambda i, k=k: i // 4 * 4 + (i + k) % 4).astype(jnp.float32)
    high = dp // 4
    other = lax.dynamic_index_in_dim(held, 1 - high, 0, keepdims=False).astype(jnp.bfloat16)
    mine = lax.dynamic_index_in_dim(held, high, 0, keepdims=False)
    mine = mine + permute(other, "dp", lambda i: (i + 4) % 8).astype(jnp.float32)
    for bit in (2, 4, 8):
        mine = mine.astype(jnp.bfloat16)
        mine = mine.astype(jnp.float32) + permute(mine, "ctx", lambda i, b=bit: i ^ b).astype(jnp.float32)
    theirs = permute(mine, "ctx", lambda i: i ^ 1)
    keys_here = core == 0
    weight_grad = jnp.stack((jnp.where(keys_here, mine, theirs), jnp.where(keys_here, theirs, mine)), axis=0)
    return (attended[None], query_grad[None], encoded_grad[None], weight_grad)


def solution(mesh):
    return jax.shard_map(
        shards,
        mesh=mesh,
        in_specs=(
            P("dp", "ctx", "nbr"),
            P("dp", "ctx", "nbr"),
            P("dp", "ctx", "nbr", None),
            P(None, None, "nbr"),
            P("dp", "ctx", None),
        ),
        out_specs=(
            P("dp", "ctx", "nbr"),
            P("dp", "ctx", "nbr"),
            P("dp", "ctx", "nbr", None),
            P(None, "dp", "nbr"),
        ),
        check_vma=False,
    )
```

```python
import math

import jax
import jax.numpy as jnp
from jax import lax
from jax.experimental import pallas as pl
from jax.experimental.pallas import tpu as pltpu
from jax.sharding import PartitionSpec as P

HEAD_DIM = 128
SPAN = 64
PART = 64
LEAD = SPAN - 1
SCALE = 1.0 / math.sqrt(HEAD_DIM)
NT = (((1,), (1,)), ((), ()))
TN = (((0,), (0,)), ((), ()))
NN = (((1,), (0,)), ((), ()))


def dot(a, b, dims):
    return lax.dot_general(a, b, dims, preferred_element_type=jnp.float32)


def attention_kernel(slots, heads, piece, units_ref, q_ref, g_ref, *refs):
    kv_refs = refs[:slots]
    att_ref, dq_ref = refs[slots : slots + 2]
    dkv_refs = refs[slots + 2 :]
    width = heads * HEAD_DIM
    spans = q_ref.shape[0] // SPAN
    for j in range(spans):
        starts = [pl.multiple_of(units_ref[j * 4 + r] * piece, piece) for r in range(4)]
        rows = pl.ds(j * SPAN, SPAN)
        for h in range(heads):
            cols = pl.ds(h * HEAD_DIM, HEAD_DIM)
            vcols = pl.ds(width + h * HEAD_DIM, HEAD_DIM)
            q = q_ref[rows, cols]
            g = g_ref[rows, cols]
            k = jnp.concatenate([ref[pl.ds(s, piece), cols] for s in starts for ref in kv_refs], axis=0)
            v = jnp.concatenate([ref[pl.ds(s, piece), vcols] for s in starts for ref in kv_refs], axis=0)
            scores = dot(q, k, NT) * SCALE
            top = jnp.max(scores, axis=-1, keepdims=True)
            raised = jnp.exp(scores - top)
            weights = raised / jnp.sum(raised, axis=-1, keepdims=True)
            low = weights.astype(jnp.bfloat16)
            d_weights = dot(g, v, NT)
            inner = jnp.sum(weights * d_weights, axis=-1, keepdims=True)
            d_scores = (weights * (d_weights - inner) * SCALE).astype(jnp.bfloat16)
            att_ref[rows, cols] = dot(low, v, NN).astype(jnp.bfloat16)
            dq_ref[rows, cols] = dot(d_scores, k, NN).astype(jnp.bfloat16)
            dk = dot(d_scores, q, TN).astype(jnp.bfloat16)
            dv = dot(low, g, TN).astype(jnp.bfloat16)
            for r, s in enumerate(starts):
                for n, ref in enumerate(dkv_refs):
                    at = (r * slots + n) * piece
                    ref[pl.ds(s, piece), cols] = dk[at : at + piece]
                    ref[pl.ds(s, piece), vcols] = dv[at : at + piece]


def attention(units, q, g, kvs, piece):
    slots = len(kvs)
    rows, width = q.shape
    heads = width // HEAD_DIM

    def body(*refs):
        attention_kernel(slots, heads, piece, *refs)

    vmem = pl.BlockSpec(memory_space=pltpu.VMEM)
    return pl.pallas_call(
        body,
        out_shape=[jax.ShapeDtypeStruct((rows, width), jnp.bfloat16)] * 2
        + [jax.ShapeDtypeStruct(kv.shape, jnp.bfloat16) for kv in kvs],
        in_specs=[pl.BlockSpec(memory_space=pltpu.SMEM)] + [vmem] * (2 + slots),
        out_specs=[vmem] * (2 + slots),
        compiler_params=pltpu.CompilerParams(vmem_limit_bytes=48 * 1024 * 1024),
        name="attention",
    )(units, q, g, *kvs)


def weight_kernel(slots, blocks, half, core_ref, *refs):
    x_refs, d_refs = refs[:slots], refs[slots : 2 * slots]
    width = d_refs[0].shape[1] // 2
    core = core_ref[0]
    start = pl.multiple_of((core if half else 1 - core) * width, width)
    for b in range(blocks):
        cols = pl.ds(b * 128, 128)
        yield cols, sum(dot(x[:, cols], d[:, pl.ds(start, width)], TN) for x, d in zip(x_refs, d_refs))


def weight_sent(core, xs, ds):
    slots, enc_width, width = len(xs), xs[0].shape[1], ds[0].shape[1] // 2

    def body(core_ref, *refs):
        for rows, term in weight_kernel(slots, enc_width // 128, False, core_ref, *refs):
            refs[-1][rows, :] = term.astype(jnp.bfloat16)

    vmem = pl.BlockSpec(memory_space=pltpu.VMEM)
    return pl.pallas_call(
        body,
        out_shape=jax.ShapeDtypeStruct((enc_width, width), jnp.bfloat16),
        in_specs=[pl.BlockSpec(memory_space=pltpu.SMEM)] + [vmem] * (2 * slots),
        out_specs=vmem,
        compiler_params=pltpu.CompilerParams(vmem_limit_bytes=48 * 1024 * 1024),
        name="weight_sent",
    )(core, *xs, *ds)


def weight_kept(core, xs, ds, away):
    slots, enc_width, width = len(xs), xs[0].shape[1], ds[0].shape[1] // 2
    rows = enc_width // 8

    def body(core_ref, *refs):
        away_ref, own_ref, *send_refs, total = refs[2 * slots :]
        for at, term in weight_kernel(slots, enc_width // 128, True, core_ref, *refs[: 2 * slots]):
            total[at, :] = term + away_ref[at, :].astype(jnp.float32)
        x = core_ref[1]
        for high in range(2):
            at = pl.multiple_of((high * 4 + x) * rows, 16)
            own_ref[high] = total[pl.ds(at, rows), :]
            for k in (1, 2, 3):
                at = pl.multiple_of((high * 4 + lax.rem(x + k, 4)) * rows, 16)
                send_refs[k - 1][high] = total[pl.ds(at, rows), :].astype(jnp.bfloat16)

    vmem = pl.BlockSpec(memory_space=pltpu.VMEM)
    return pl.pallas_call(
        body,
        out_shape=[jax.ShapeDtypeStruct((2, rows, width), jnp.float32)]
        + [jax.ShapeDtypeStruct((2, rows, width), jnp.bfloat16)] * 3,
        in_specs=[pl.BlockSpec(memory_space=pltpu.SMEM)] + [vmem] * (2 * slots + 1),
        out_specs=[vmem] * 4,
        scratch_shapes=[pltpu.VMEM((enc_width, width), jnp.float32)],
        compiler_params=pltpu.CompilerParams(vmem_limit_bytes=48 * 1024 * 1024),
        name="weight_kept",
    )(core, *xs, *ds, away)


def permute(x, axis, to):
    n = lax.axis_size(axis)
    return lax.ppermute(x, axis, [(i, to(i)) for i in range(n) if 0 <= to(i) < n])


def exchange(x):
    return lax.all_to_all(x, "ctx", split_axis=0, concat_axis=0, tiled=True)


def pair(x, bit):
    return permute(x, "nbr", lambda i: i ^ bit)


def add(a, b):
    return (a.astype(jnp.float32) + b.astype(jnp.float32)).astype(jnp.bfloat16)


def shards(queries, cotangent, encoded, kv_weight, neighbour_ids):
    q, g, enc = queries[0], cotangent[0], encoded[0]
    tokens, width = q.shape
    units, piece, enc_width = enc.shape
    half = piece // 2
    flat = (units * piece, enc_width)
    ctx = lax.axis_index("ctx")
    dp = lax.axis_index("dp")
    joined = jnp.concatenate((kv_weight[0], kv_weight[1]), axis=1)

    enc_a, enc_b = enc[:, :half], enc[:, half:]
    own_a = exchange(enc_a)
    b_02 = exchange(jnp.concatenate((enc_b, pair(enc_b, 2)), axis=1)).reshape(flat)
    a_02 = jnp.concatenate((own_a, pair(own_a, 2)), axis=1).reshape(flat)
    a_13 = pair(a_02, 1)
    b_13 = pair(b_02, 1)
    xs = [a_02, b_02, a_13, b_13]
    kvs = [dot(x, joined, NN).astype(jnp.bfloat16) for x in xs]

    head = jnp.concatenate((q[:LEAD], g[:LEAD]), axis=1)
    ahead = permute(head, "ctx", lambda i: i - 1)
    q_rows = jnp.concatenate((q[LEAD:], ahead[:, :width]), axis=0)
    g_rows = jnp.concatenate((g[LEAD:], ahead[:, width:]), axis=0)

    unit_of = (neighbour_ids[0] // units).reshape(-1)
    att, dq, *ds = attention(unit_of, q_rows, g_rows, kvs, piece)

    p_a02, p_b02, p_a13, p_b13 = [dot(d, joined, NT).astype(jnp.bfloat16) for d in ds]
    s_b = add(p_b02, pair(p_b13, 1)).reshape(units, piece, enc_width)
    s_a = add(p_a02, pair(p_a13, 1)).reshape(units, piece, enc_width)
    back_b = exchange(s_b)
    grad_b = add(back_b[:, :half], pair(back_b[:, half:], 2))
    grad_a = exchange(add(s_a[:, :half], pair(s_a[:, half:], 2)))
    encoded_grad = jnp.concatenate((grad_a, grad_b), axis=1)

    tail = jnp.concatenate((att[tokens - LEAD :], dq[tokens - LEAD :]), axis=1)
    behind = permute(tail, "ctx", lambda i: i + 1)
    attended = jnp.concatenate((behind[:, :width], att[: tokens - LEAD]), axis=0)
    query_grad = jnp.concatenate((behind[:, width:], dq[: tokens - LEAD]), axis=0)

    core = ctx % 2
    place = jnp.stack((core, dp % 4)).astype(jnp.int32)
    away = permute(weight_sent(place, xs, ds), "ctx", lambda i: i ^ 1)
    held, *sends = weight_kept(place, xs, ds, away)
    for k in (1, 3, 2):
        held = held + permute(sends[k - 1], "dp", lambda i, k=k: i // 4 * 4 + (i + k) % 4).astype(jnp.float32)
    high = dp // 4
    other = lax.dynamic_index_in_dim(held, 1 - high, 0, keepdims=False).astype(jnp.bfloat16)
    mine = lax.dynamic_index_in_dim(held, high, 0, keepdims=False)
    mine = mine + permute(other, "dp", lambda i: (i + 4) % 8).astype(jnp.float32)
    for bit in (2, 4, 8):
        mine = mine.astype(jnp.bfloat16)
        mine = mine.astype(jnp.float32) + permute(mine, "ctx", lambda i, b=bit: i ^ b).astype(jnp.float32)
    theirs = permute(mine, "ctx", lambda i: i ^ 1)
    keys_here = core == 0
    weight_grad = jnp.stack((jnp.where(keys_here, mine, theirs), jnp.where(keys_here, theirs, mine)), axis=0)
    return (attended[None], query_grad[None], encoded_grad[None], weight_grad)


def solution(mesh):
    return jax.shard_map(
        shards,
        mesh=mesh,
        in_specs=(
            P("dp", "ctx", "nbr"),
            P("dp", "ctx", "nbr"),
            P("dp", "ctx", "nbr", None),
            P(None, None, "nbr"),
            P("dp", "ctx", None),
        ),
        out_specs=(
            P("dp", "ctx", "nbr"),
            P("dp", "ctx", "nbr"),
            P("dp", "ctx", "nbr", None),
            P(None, "dp", "nbr"),
        ),
        check_vma=False,
    )
```

```python
import math

import jax
import jax.numpy as jnp
from jax import lax
from jax.experimental import pallas as pl
from jax.experimental.pallas import tpu as pltpu
from jax.sharding import PartitionSpec as P

HEAD_DIM = 128
SPAN = 64
PART = 64
LEAD = SPAN - 1
SCALE = 1.0 / math.sqrt(HEAD_DIM)
NT = (((1,), (1,)), ((), ()))
TN = (((0,), (0,)), ((), ()))
NN = (((1,), (0,)), ((), ()))
VMEM = pl.BlockSpec(memory_space=pltpu.VMEM)
SMEM = pl.BlockSpec(memory_space=pltpu.SMEM)
PARAMS = pltpu.CompilerParams(vmem_limit_bytes=50 * 1024 * 1024)


def dot(a, b, dims):
    return lax.dot_general(a, b, dims, preferred_element_type=jnp.float32)


def span_rows(own, ahead):
    own, ahead = own.astype(jnp.float32), ahead.astype(jnp.float32)
    row = lax.broadcasted_iota(jnp.int32, ahead.shape, 0)
    mixed = jnp.concatenate((jnp.where(row < LEAD, ahead, own[:SPAN]), own[SPAN:]), axis=0)
    return pltpu.roll(mixed, own.shape[0] - LEAD, 0).astype(jnp.bfloat16)


def block_body(slots, units, piece, units_ref, place_ref, q_ref, g_ref, ahead_ref, w_ref, *refs):
    xa_refs, xb_ref = refs[:slots], refs[slots]
    att_ref, dq_ref, *p_refs = refs[slots + 1 : 2 * slots + 3]
    sent_ref, kept_ref, xa, key, value, grad, q_rows, g_rows, att, dq = refs[2 * slots + 3 :]
    tokens, width = q_ref.shape
    first = xa.shape[1]
    enc_width = w_ref.shape[1]
    heads = width // HEAD_DIM
    for n, ref in enumerate(xa_refs):
        for u in range(units):
            xa[u * PART + n * piece : u * PART + (n + 1) * piece, :] = ref[u * piece : (u + 1) * piece, :]
    chunk = 4 * PART
    for c in range(units // 4):
        rows = pl.ds(c * chunk, chunk)
        for kind, out in enumerate((key, value)):
            term = dot(xa[rows, :], w_ref[kind, :first, :], NN) + dot(xb_ref[rows, :], w_ref[kind, first:, :], NN)
            out[rows, :] = term.astype(jnp.bfloat16)
    for h in range(heads):
        cols = pl.ds(h * HEAD_DIM, HEAD_DIM)
        q_rows[:, cols] = span_rows(q_ref[:, cols], ahead_ref[:, cols])
        g_rows[:, cols] = span_rows(g_ref[:, cols], ahead_ref[:, pl.ds(width + h * HEAD_DIM, HEAD_DIM)])
    for j in range(tokens // SPAN):
        starts = [pl.multiple_of(units_ref[j * 4 + r] * PART, PART) for r in range(4)]
        rows = pl.ds(j * SPAN, SPAN)
        for h in range(heads):
            cols = pl.ds(h * HEAD_DIM, HEAD_DIM)
            q = q_rows[rows, cols]
            g = g_rows[rows, cols]
            k = jnp.concatenate([key[pl.ds(s, PART), cols] for s in starts], axis=0)
            v = jnp.concatenate([value[pl.ds(s, PART), cols] for s in starts], axis=0)
            scores = dot(q, k, NT) * SCALE
            raised = jnp.exp(scores - jnp.max(scores, axis=-1, keepdims=True))
            weights = raised / jnp.sum(raised, axis=-1, keepdims=True)
            low = weights.astype(jnp.bfloat16)
            d_weights = dot(g, v, NT)
            inner = jnp.sum(weights * d_weights, axis=-1, keepdims=True)
            d_scores = (weights * (d_weights - inner) * SCALE).astype(jnp.bfloat16)
            att[rows, cols] = dot(low, v, NN)
            dq[rows, cols] = dot(d_scores, k, NN)
            dk = dot(d_scores, q, TN).astype(jnp.bfloat16)
            dv = dot(low, g, TN).astype(jnp.bfloat16)
            for r, s in enumerate(starts):
                grad[0, pl.ds(s, PART), cols] = dk[r * PART : (r + 1) * PART]
                grad[1, pl.ds(s, PART), cols] = dv[r * PART : (r + 1) * PART]
    for h in range(heads):
        cols = pl.ds(h * HEAD_DIM, HEAD_DIM)
        att_ref[:, cols] = pltpu.roll(att[:, cols], LEAD, 0).astype(jnp.bfloat16)
        dq_ref[:, cols] = pltpu.roll(dq[:, cols], LEAD, 0).astype(jnp.bfloat16)
    for c in range(units // 4):
        rows = pl.ds(c * chunk, chunk)
        term = dot(grad[0, rows, :], w_ref[0], NT) + dot(grad[1, rows, :], w_ref[1], NT)
        term = term.astype(jnp.bfloat16)
        for u in range(4):
            for n, ref in enumerate(p_refs):
                at = u * PART + n * piece
                ref[(c * 4 + u) * piece : (c * 4 + u + 1) * piece, :] = term[at : at + piece]
    core = place_ref[0]
    for e in range(0, enc_width, 128):
        x = xa[:, e : e + 128] if e < first else xb_ref[:, e - first : e - first + 128]
        x = x.T
        sent_ref[e : e + 128, :] = dot(x, grad[1 - core], NN).astype(jnp.bfloat16)
        kept_ref[e : e + 128, :] = dot(x, grad[core], NN)


def block(units_of, place, q, g, ahead, w, xa, xb):
    slots = len(xa)
    tokens, width = q.shape
    first = xa[0].shape[1]
    enc_width = w.shape[1]
    all_rows = xb.shape[0]
    units, piece = all_rows // PART, PART // slots

    def body(*refs):
        block_body(slots, units, piece, *refs)

    def low(*shape):
        return jax.ShapeDtypeStruct(shape, jnp.bfloat16)

    return pl.pallas_call(
        body,
        out_shape=[low(tokens, width)] * 2
        + [low(units * piece, enc_width)] * slots
        + [low(enc_width, width), jax.ShapeDtypeStruct((enc_width, width), jnp.float32)],
        in_specs=[SMEM] * 2 + [VMEM] * (5 + slots),
        out_specs=[VMEM] * (4 + slots),
        scratch_shapes=[
            pltpu.VMEM((all_rows, first), jnp.bfloat16),
            pltpu.VMEM((all_rows, width), jnp.bfloat16),
            pltpu.VMEM((all_rows, width), jnp.bfloat16),
            pltpu.VMEM((2, all_rows, width), jnp.bfloat16),
            pltpu.VMEM((tokens, width), jnp.bfloat16),
            pltpu.VMEM((tokens, width), jnp.bfloat16),
            pltpu.VMEM((tokens, width), jnp.float32),
            pltpu.VMEM((tokens, width), jnp.float32),
        ],
        compiler_params=PARAMS,
        name="block",
    )(units_of, place, q, g, ahead, w, *xa, xb)


def cut(place, kept, away):
    enc_width, width = kept.shape
    rows = enc_width // 8

    def body(place_ref, kept_ref, away_ref, own_ref, *send_refs):
        x = place_ref[1]
        for high in range(2):
            for k in range(4):
                at = pl.multiple_of((high * 4 + lax.rem(x + k, 4)) * rows, 16)
                term = kept_ref[pl.ds(at, rows), :] + away_ref[pl.ds(at, rows), :].astype(jnp.float32)
                if k:
                    send_refs[k - 1][high] = term.astype(jnp.bfloat16)
                else:
                    own_ref[high] = term

    return pl.pallas_call(
        body,
        out_shape=[jax.ShapeDtypeStruct((2, rows, width), jnp.float32)]
        + [jax.ShapeDtypeStruct((2, rows, width), jnp.bfloat16)] * 3,
        in_specs=[SMEM] + [VMEM] * 2,
        out_specs=[VMEM] * 4,
        compiler_params=PARAMS,
        name="cut",
    )(place, kept, away)


def fold(place, own, parts, partial, terms):
    _, rows, width = own.shape

    def body(place_ref, own_ref, *refs):
        part_refs, partial_ref, term_refs = refs[:3], refs[3], refs[4:7]
        mine_ref, other_ref, total_ref = refs[7:]
        high = place_ref[2]
        for ref, at in ((mine_ref, high), (other_ref, 1 - high)):
            total = own_ref[at]
            for part in part_refs:
                total = total + part[at].astype(jnp.float32)
            ref[...] = total.astype(ref.dtype)
        total = partial_ref[...].astype(jnp.float32)
        for term in term_refs:
            total = total + term[...].astype(jnp.float32)
        total_ref[...] = total.astype(jnp.bfloat16)

    return pl.pallas_call(
        body,
        out_shape=[
            jax.ShapeDtypeStruct((rows, width), jnp.float32),
            jax.ShapeDtypeStruct((rows, width), jnp.bfloat16),
            jax.ShapeDtypeStruct(partial.shape, jnp.bfloat16),
        ],
        in_specs=[SMEM] + [VMEM] * 8,
        out_specs=[VMEM] * 3,
        compiler_params=PARAMS,
        name="fold",
    )(place, own, *parts, partial, *terms)


def permute(x, axis, to):
    n = lax.axis_size(axis)
    return lax.ppermute(x, axis, [(i, to(i)) for i in range(n) if 0 <= to(i) < n])


def exchange(x):
    return lax.all_to_all(x, "ctx", split_axis=0, concat_axis=0, tiled=True)


def shards(queries, cotangent, encoded, kv_weight, neighbour_ids):
    q, g, enc = queries[0], cotangent[0], encoded[0]
    width = q.shape[1]
    units, piece, enc_width = enc.shape
    groups = lax.axis_size("nbr")
    ctx = lax.axis_index("ctx")
    dp = lax.axis_index("dp")
    place = jnp.stack((ctx % 2, dp % 4, dp // 4)).astype(jnp.int32)

    def gathered(x):
        return [x] + [permute(x, "nbr", lambda i, k=k: (i + k) % groups) for k in range(1, groups)]

    first = enc_width // 7 * 5
    xa = gathered(exchange(enc[:, :, :first]).reshape(units * piece, first))
    xb = exchange(jnp.concatenate(gathered(enc[:, :, first:]), axis=1)).reshape(-1, enc_width - first)

    head = jnp.concatenate((q[:SPAN], g[:SPAN]), axis=1)
    ahead = permute(head, "ctx", lambda i: i - 1)

    unit_of = (neighbour_ids[0] // units).reshape(-1)
    att, dq, *partials, sent, kept = block(unit_of, place, q, g, ahead, kv_weight, xa, xb)

    away = permute(sent, "ctx", lambda i: i ^ 1)
    own, *sends = cut(place, kept, away)
    parts = [
        permute(sends[k - 1], "dp", lambda i, k=k: i // 4 * 4 + (i + k) % 4) for k in (1, 2, 3)
    ]
    terms = [permute(partials[k], "nbr", lambda i, k=k: (i - k) % groups) for k in range(1, groups)]
    mine, other, total = fold(place, own, parts, partials[0], terms)
    encoded_grad = exchange(total.reshape(units, piece, enc_width))
    mine = mine + permute(other, "dp", lambda i: (i + 4) % 8).astype(jnp.float32)
    low = mine.astype(jnp.bfloat16)
    low = add(low, permute(low, "ctx", lambda i: i ^ 2)).astype(jnp.bfloat16)
    by = [permute(low, "ctx", lambda i, b=b: i ^ b) for b in (4, 8, 12)]
    mine = add(low, by[0]) + add(by[1], by[2])
    theirs = permute(mine, "ctx", lambda i: i ^ 1)
    keys_here = ctx % 2 == 0
    weight_grad = jnp.stack((jnp.where(keys_here, mine, theirs), jnp.where(keys_here, theirs, mine)), axis=0)

    tail = jnp.concatenate((att[:SPAN], dq[:SPAN]), axis=1)
    behind = permute(tail, "ctx", lambda i: i + 1)
    lead = lax.broadcasted_iota(jnp.int32, (SPAN, width), 0) < LEAD
    attended = jnp.concatenate((jnp.where(lead, behind[:, :width], att[:SPAN]), att[SPAN:]), axis=0)
    query_grad = jnp.concatenate((jnp.where(lead, behind[:, width:], dq[:SPAN]), dq[SPAN:]), axis=0)
    return (attended[None], query_grad[None], encoded_grad[None], weight_grad)


def add(a, b):
    return a.astype(jnp.float32) + b.astype(jnp.float32)


def solution(mesh):
    return jax.shard_map(
        shards,
        mesh=mesh,
        in_specs=(
            P("dp", "ctx", "nbr"),
            P("dp", "ctx", "nbr"),
            P("dp", "ctx", "nbr", None),
            P(None, None, "nbr"),
            P("dp", "ctx", None),
        ),
        out_specs=(
            P("dp", "ctx", "nbr"),
            P("dp", "ctx", "nbr"),
            P("dp", "ctx", "nbr", None),
            P(None, "dp", "nbr"),
        ),
        check_vma=False,
    )
```

```python
import math

import jax
import jax.numpy as jnp
from jax import lax
from jax.experimental import pallas as pl
from jax.experimental.pallas import tpu as pltpu
from jax.sharding import PartitionSpec as P

HEAD_DIM = 128
SPAN = 64
PART = 64
LEAD = SPAN - 1
SCALE = 1.0 / math.sqrt(HEAD_DIM)
NT = (((1,), (1,)), ((), ()))
TN = (((0,), (0,)), ((), ()))
NN = (((1,), (0,)), ((), ()))
VMEM = pl.BlockSpec(memory_space=pltpu.VMEM)
SMEM = pl.BlockSpec(memory_space=pltpu.SMEM)
PARAMS = pltpu.CompilerParams(vmem_limit_bytes=50 * 1024 * 1024)


def dot(a, b, dims):
    return lax.dot_general(a, b, dims, preferred_element_type=jnp.float32)


def span_rows(own, ahead):
    own, ahead = own.astype(jnp.float32), ahead.astype(jnp.float32)
    row = lax.broadcasted_iota(jnp.int32, ahead.shape, 0)
    mixed = jnp.concatenate((jnp.where(row < LEAD, ahead, own[:SPAN]), own[SPAN:]), axis=0)
    return pltpu.roll(mixed, own.shape[0] - LEAD, 0).astype(jnp.bfloat16)


def block_body(
    units_ref, place_ref, q_ref, g_ref, ahead_ref, w_ref, x_ref, att_ref, dq_ref, partial_ref, sent_ref, kept_ref,
    key, value, grad, q_rows, g_rows, att, dq,
):
    tokens, width = q_ref.shape
    all_rows, enc_width = x_ref.shape
    heads = width // HEAD_DIM
    chunk = 4 * PART
    for c in range(all_rows // chunk):
        rows = pl.ds(c * chunk, chunk)
        for kind, out in enumerate((key, value)):
            out[rows, :] = dot(x_ref[rows, :], w_ref[kind], NN).astype(jnp.bfloat16)
    for h in range(heads):
        cols = pl.ds(h * HEAD_DIM, HEAD_DIM)
        q_rows[:, cols] = span_rows(q_ref[:, cols], ahead_ref[:, cols])
        g_rows[:, cols] = span_rows(g_ref[:, cols], ahead_ref[:, pl.ds(width + h * HEAD_DIM, HEAD_DIM)])
    for j in range(tokens // SPAN):
        starts = [pl.multiple_of(units_ref[j * 4 + r] * PART, PART) for r in range(4)]
        rows = pl.ds(j * SPAN, SPAN)
        for h in range(heads):
            cols = pl.ds(h * HEAD_DIM, HEAD_DIM)
            q = q_rows[rows, cols]
            g = g_rows[rows, cols]
            k = jnp.concatenate([key[pl.ds(s, PART), cols] for s in starts], axis=0)
            v = jnp.concatenate([value[pl.ds(s, PART), cols] for s in starts], axis=0)
            scores = dot(q, k, NT) * SCALE
            raised = jnp.exp(scores - jnp.max(scores, axis=-1, keepdims=True))
            weights = raised / jnp.sum(raised, axis=-1, keepdims=True)
            low = weights.astype(jnp.bfloat16)
            d_weights = dot(g, v, NT)
            inner = jnp.sum(weights * d_weights, axis=-1, keepdims=True)
            d_scores = (weights * (d_weights - inner) * SCALE).astype(jnp.bfloat16)
            att[rows, cols] = dot(low, v, NN)
            dq[rows, cols] = dot(d_scores, k, NN)
            dk = dot(d_scores, q, TN).astype(jnp.bfloat16)
            dv = dot(low, g, TN).astype(jnp.bfloat16)
            for r, s in enumerate(starts):
                grad[0, pl.ds(s, PART), cols] = dk[r * PART : (r + 1) * PART]
                grad[1, pl.ds(s, PART), cols] = dv[r * PART : (r + 1) * PART]
    for h in range(heads):
        cols = pl.ds(h * HEAD_DIM, HEAD_DIM)
        att_ref[:, cols] = pltpu.roll(att[:, cols], LEAD, 0).astype(jnp.bfloat16)
        dq_ref[:, cols] = pltpu.roll(dq[:, cols], LEAD, 0).astype(jnp.bfloat16)
    for c in range(all_rows // chunk):
        rows = pl.ds(c * chunk, chunk)
        term = dot(grad[0, rows, :], w_ref[0], NT) + dot(grad[1, rows, :], w_ref[1], NT)
        partial_ref[rows, :] = term.astype(jnp.bfloat16)
    core = place_ref[0]
    for e in range(0, enc_width, 128):
        x = x_ref[:, e : e + 128].T
        sent_ref[e : e + 128, :] = dot(x, grad[1 - core], NN).astype(jnp.bfloat16)
        kept_ref[e : e + 128, :] = dot(x, grad[core], NN)


def block(units_of, place, q, g, ahead, w, x):
    tokens, width = q.shape
    all_rows, enc_width = x.shape

    def low(*shape):
        return jax.ShapeDtypeStruct(shape, jnp.bfloat16)

    return pl.pallas_call(
        block_body,
        out_shape=[
            low(tokens, width),
            low(tokens, width),
            low(all_rows, enc_width),
            low(enc_width, width),
            jax.ShapeDtypeStruct((enc_width, width), jnp.float32),
        ],
        in_specs=[SMEM] * 2 + [VMEM] * 5,
        out_specs=[VMEM] * 5,
        scratch_shapes=[
            pltpu.VMEM((all_rows, width), jnp.bfloat16),
            pltpu.VMEM((all_rows, width), jnp.bfloat16),
            pltpu.VMEM((2, all_rows, width), jnp.bfloat16),
            pltpu.VMEM((tokens, width), jnp.bfloat16),
            pltpu.VMEM((tokens, width), jnp.bfloat16),
            pltpu.VMEM((tokens, width), jnp.float32),
            pltpu.VMEM((tokens, width), jnp.float32),
        ],
        compiler_params=PARAMS,
        name="block",
    )(units_of, place, q, g, ahead, w, x)


def cut(place, kept, away, att, dq, behind):
    enc_width, width = kept.shape
    rows = enc_width // 8

    def body(place_ref, kept_ref, away_ref, att_ref, dq_ref, behind_ref, own_ref, *refs):
        send_refs, full_refs = refs[:3], refs[3:]
        x = place_ref[1]
        for high in range(2):
            for k in range(4):
                at = pl.multiple_of((high * 4 + lax.rem(x + k, 4)) * rows, 16)
                term = kept_ref[pl.ds(at, rows), :] + away_ref[pl.ds(at, rows), :].astype(jnp.float32)
                if k:
                    send_refs[k - 1][high] = term.astype(jnp.bfloat16)
                else:
                    own_ref[high] = term
        lead = lax.broadcasted_iota(jnp.int32, (SPAN, width), 0) < LEAD
        for n, (ref, full) in enumerate(zip((att_ref, dq_ref), full_refs)):
            came = behind_ref[:, n * width : (n + 1) * width].astype(jnp.float32)
            full[:SPAN, :] = jnp.where(lead, came, ref[:SPAN, :].astype(jnp.float32)).astype(jnp.bfloat16)
            full[SPAN:, :] = ref[SPAN:, :]

    return pl.pallas_call(
        body,
        out_shape=[jax.ShapeDtypeStruct((2, rows, width), jnp.float32)]
        + [jax.ShapeDtypeStruct((2, rows, width), jnp.bfloat16)] * 3
        + [jax.ShapeDtypeStruct(att.shape, jnp.bfloat16)] * 2,
        in_specs=[SMEM] + [VMEM] * 5,
        out_specs=[VMEM] * 6,
        compiler_params=PARAMS,
        name="cut",
    )(place, kept, away, att, dq, behind)


def permute(x, axis, to):
    n = lax.axis_size(axis)
    return lax.ppermute(x, axis, [(i, to(i)) for i in range(n) if 0 <= to(i) < n])


def exchange(x):
    outer, inner, *rest = x.shape
    x = lax.all_to_all(x.reshape(outer * inner, *rest), ("ctx", "nbr"), split_axis=0, concat_axis=0, tiled=True)
    return x.reshape(outer, inner, *rest)


def shards(queries, cotangent, encoded, kv_weight, neighbour_ids):
    q, g, enc = queries[0], cotangent[0], encoded[0]
    units, piece, enc_width = enc.shape
    groups = lax.axis_size("nbr")
    ctx = lax.axis_index("ctx")
    dp = lax.axis_index("dp")
    place = jnp.stack((ctx % 2, dp % 4, dp // 4)).astype(jnp.int32)

    copies = jnp.broadcast_to(enc[:, None], (units, groups, piece, enc_width))
    x = exchange(copies).reshape(units * PART, enc_width)

    head = jnp.concatenate((q[:SPAN], g[:SPAN]), axis=1)
    ahead = permute(head, "ctx", lambda i: i - 1)

    unit_of = (neighbour_ids[0] // units).reshape(-1)
    att, dq, partial, sent, kept = block(unit_of, place, q, g, ahead, kv_weight, x)

    terms = exchange(partial.reshape(units, groups, piece, enc_width))
    encoded_grad = jnp.sum(terms.astype(jnp.float32), axis=1).astype(jnp.bfloat16)

    away = permute(sent, "ctx", lambda i: i ^ 1)
    tail = jnp.concatenate((att[:SPAN], dq[:SPAN]), axis=1)
    behind = permute(tail, "ctx", lambda i: i + 1)
    held, *sends, attended, query_grad = cut(place, kept, away, att, dq, behind)
    for k in (1, 3, 2):
        held = add(held, permute(sends[k - 1], "dp", lambda i, k=k: i // 4 * 4 + (i + k) % 4))
    high = dp // 4
    other = lax.dynamic_index_in_dim(held, 1 - high, 0, keepdims=False).astype(jnp.bfloat16)
    mine = lax.dynamic_index_in_dim(held, high, 0, keepdims=False)
    low = add(mine, permute(other, "dp", lambda i: (i + 4) % 8)).astype(jnp.bfloat16)
    low = add(low, permute(low, "ctx", lambda i: i ^ 2)).astype(jnp.bfloat16)
    by = [permute(low, "ctx", lambda i, b=b: i ^ b) for b in (4, 8, 12)]
    mine = add(low, by[0]) + add(by[1], by[2])
    theirs = permute(mine, "ctx", lambda i: i ^ 1)
    keys_here = ctx % 2 == 0
    weight_grad = jnp.stack((jnp.where(keys_here, mine, theirs), jnp.where(keys_here, theirs, mine)), axis=0)
    return (attended[None], query_grad[None], encoded_grad[None], weight_grad)


def add(a, b):
    return a.astype(jnp.float32) + b.astype(jnp.float32)


def solution(mesh):
    return jax.shard_map(
        shards,
        mesh=mesh,
        in_specs=(
            P("dp", "ctx", "nbr"),
            P("dp", "ctx", "nbr"),
            P("dp", "ctx", "nbr", None),
            P(None, None, "nbr"),
            P("dp", "ctx", None),
        ),
        out_specs=(
            P("dp", "ctx", "nbr"),
            P("dp", "ctx", "nbr"),
            P("dp", "ctx", "nbr", None),
            P(None, "dp", "nbr"),
        ),
        check_vma=False,
    )
```

```python
import math

import jax
import jax.numpy as jnp
from jax import lax
from jax.experimental import pallas as pl
from jax.experimental.pallas import tpu as pltpu
from jax.sharding import PartitionSpec as P

HEAD_DIM = 128
SPAN = 64
PART = 64
LEAD = SPAN - 1
SCALE = 1.0 / math.sqrt(HEAD_DIM)
NT = (((1,), (1,)), ((), ()))
TN = (((0,), (0,)), ((), ()))
NN = (((1,), (0,)), ((), ()))
VMEM = pl.BlockSpec(memory_space=pltpu.VMEM)
SMEM = pl.BlockSpec(memory_space=pltpu.SMEM)
PARAMS = pltpu.CompilerParams(vmem_limit_bytes=50 * 1024 * 1024)


def dot(a, b, dims):
    return lax.dot_general(a, b, dims, preferred_element_type=jnp.float32)


def span_rows(own, ahead):
    own, ahead = own.astype(jnp.float32), ahead.astype(jnp.float32)
    row = lax.broadcasted_iota(jnp.int32, ahead.shape, 0)
    mixed = jnp.concatenate((jnp.where(row < LEAD, ahead, own[:SPAN]), own[SPAN:]), axis=0)
    return pltpu.roll(mixed, own.shape[0] - LEAD, 0).astype(jnp.bfloat16)


def block_body(
    units_ref, q_ref, g_ref, ahead_ref, w_ref, x_ref, att_ref, dq_ref, grad, *refs
):
    p_refs = refs[:-7]
    key, value, q_rows, g_rows, att, dq, spare = refs[-7:]
    nbr = units_ref[units_ref.shape[0] - 1]
    tokens, width = q_ref.shape
    all_rows = x_ref.shape[0]
    piece = PART // len(p_refs)
    heads = width // HEAD_DIM
    chunk = 4 * PART
    for c in range(all_rows // chunk):
        rows = pl.ds(c * chunk, chunk)
        for kind, out in enumerate((key, value)):
            out[rows, :] = dot(x_ref[rows, :], w_ref[kind], NN).astype(jnp.bfloat16)
    for h in range(heads):
        cols = pl.ds(h * HEAD_DIM, HEAD_DIM)
        q_rows[:, cols] = span_rows(q_ref[:, cols], ahead_ref[:, cols])
        g_rows[:, cols] = span_rows(g_ref[:, cols], ahead_ref[:, pl.ds(width + h * HEAD_DIM, HEAD_DIM)])
    for j in range(tokens // SPAN):
        starts = [pl.multiple_of(units_ref[j * 4 + r] * PART, PART) for r in range(4)]
        rows = pl.ds(j * SPAN, SPAN)
        for h in range(heads):
            cols = pl.ds(h * HEAD_DIM, HEAD_DIM)
            q = q_rows[rows, cols]
            g = g_rows[rows, cols]
            k = jnp.concatenate([key[pl.ds(s, PART), cols] for s in starts], axis=0)
            v = jnp.concatenate([value[pl.ds(s, PART), cols] for s in starts], axis=0)
            scores = dot(q, k, NT) * SCALE
            raised = jnp.exp(scores - jnp.max(scores, axis=-1, keepdims=True))
            weights = raised / jnp.sum(raised, axis=-1, keepdims=True)
            low = weights.astype(jnp.bfloat16)
            d_weights = dot(g, v, NT)
            inner = jnp.sum(weights * d_weights, axis=-1, keepdims=True)
            d_scores = (weights * (d_weights - inner) * SCALE).astype(jnp.bfloat16)
            att[rows, cols] = dot(low, v, NN)
            dq[rows, cols] = dot(d_scores, k, NN)
            dk = dot(d_scores, q, TN).astype(jnp.bfloat16)
            dv = dot(low, g, TN).astype(jnp.bfloat16)
            for r, s in enumerate(starts):
                grad[0, pl.ds(s, PART), cols] = dk[r * PART : (r + 1) * PART]
                grad[1, pl.ds(s, PART), cols] = dv[r * PART : (r + 1) * PART]
    for h in range(heads):
        cols = pl.ds(h * HEAD_DIM, HEAD_DIM)
        att_ref[:, cols] = pltpu.roll(att[:, cols], LEAD, 0).astype(jnp.bfloat16)
        dq_ref[:, cols] = pltpu.roll(dq[:, cols], LEAD, 0).astype(jnp.bfloat16)
    for c in range(all_rows // chunk):
        rows = pl.ds(c * chunk, chunk)
        term = dot(grad[0, rows, :], w_ref[0], NT) + dot(grad[1, rows, :], w_ref[1], NT)
        spare[...] = term.astype(jnp.bfloat16)
        for n, ref in enumerate(p_refs):
            slot = lax.rem(nbr + n, len(p_refs))
            for u in range(4):
                at = pl.multiple_of(u * PART + slot * piece, piece)
                ref[(c * 4 + u) * piece : (c * 4 + u + 1) * piece, :] = spare[pl.ds(at, piece), :]


def low(*shape):
    return jax.ShapeDtypeStruct(shape, jnp.bfloat16)


def wide(*shape):
    return jax.ShapeDtypeStruct(shape, jnp.float32)


def call(body, name, out_shape, scratch, place, *args):
    return pl.pallas_call(
        body,
        out_shape=out_shape,
        in_specs=[SMEM] + [VMEM] * len(args),
        out_specs=jax.tree.map(lambda _: VMEM, out_shape),
        scratch_shapes=scratch,
        compiler_params=PARAMS,
        name=name,
    )(place, *args)


def block(slots, units_of, q, g, ahead, w, x):
    tokens, width = q.shape
    all_rows, enc_width = x.shape
    out_shape = [low(tokens, width), low(tokens, width), low(2, all_rows, width)]
    out_shape += [low(all_rows // slots, enc_width)] * slots
    scratch = [pltpu.VMEM((all_rows, width), jnp.bfloat16)] * 2
    scratch += [pltpu.VMEM((tokens, width), jnp.bfloat16)] * 2
    scratch += [pltpu.VMEM((tokens, width), jnp.float32)] * 2 + [pltpu.VMEM((4 * PART, enc_width), jnp.bfloat16)]
    return call(block_body, "block", out_shape, scratch, units_of, q, g, ahead, w, x)


def products(place, x, grad):
    enc_width, width = x.shape[1], grad.shape[2]

    def body(place_ref, x_ref, grad_ref, sent_ref, kept_ref):
        core = place_ref[0]
        for e in range(0, enc_width, 128):
            part = x_ref[:, e : e + 128].T
            sent_ref[e : e + 128, :] = dot(part, grad_ref[1 - core], NN).astype(jnp.bfloat16)
            kept_ref[e : e + 128, :] = dot(part, grad_ref[core], NN)

    return call(body, "products", [low(enc_width, width), wide(enc_width, width)], [], place, x, grad)


def cut(place, kept, away, att, dq, behind):
    enc_width, width = kept.shape
    rows = enc_width // 8

    def body(place_ref, kept_ref, away_ref, att_ref, dq_ref, behind_ref, own_ref, *refs):
        send_refs, full_refs = refs[:3], refs[3:]
        x = place_ref[1]
        for high in range(2):
            for k in range(4):
                at = pl.multiple_of((high * 4 + lax.rem(x + k, 4)) * rows, 16)
                term = kept_ref[pl.ds(at, rows), :] + away_ref[pl.ds(at, rows), :].astype(jnp.float32)
                if k:
                    send_refs[k - 1][high] = term.astype(jnp.bfloat16)
                else:
                    own_ref[high] = term
        lead = lax.broadcasted_iota(jnp.int32, (SPAN, width), 0) < LEAD
        for n, (ref, full) in enumerate(zip((att_ref, dq_ref), full_refs)):
            came = behind_ref[:, n * width : (n + 1) * width].astype(jnp.float32)
            full[:SPAN, :] = jnp.where(lead, came, ref[:SPAN, :].astype(jnp.float32)).astype(jnp.bfloat16)
            full[SPAN:, :] = ref[SPAN:, :]

    out_shape = [wide(2, rows, width)] + [low(2, rows, width)] * 3 + [low(*att.shape)] * 2
    return call(body, "cut", out_shape, [], place, kept, away, att, dq, behind)


def x_sum(place, own, parts, partial, term):
    def body(_, own_ref, *refs):
        part_refs, partial_ref, term_ref, held_ref, acc_ref = refs[:3], *refs[3:]
        total = own_ref[...]
        for ref in part_refs:
            total = total + ref[...].astype(jnp.float32)
        held_ref[...] = total.astype(jnp.bfloat16)
        acc_ref[...] = add(partial_ref[...], term_ref[...])

    return call(body, "x_sum", [low(*own.shape), wide(*partial.shape)], [], place, own, *parts, partial, term)


def y_pair(place, held, came, acc, term):
    def body(_, held_ref, came_ref, acc_ref, term_ref, both_ref, out_ref):
        both_ref[...] = add(held_ref[...], came_ref[...]).astype(jnp.bfloat16)
        out_ref[...] = add(acc_ref[...], term_ref[...])

    return call(body, "y_pair", [low(*held.shape), wide(*acc.shape)], [], place, held, came, acc, term)


def fold(place, held, by, acc, term):
    _, rows, width = held.shape

    def body(place_ref, held_ref, a_ref, b_ref, c_ref, acc_ref, term_ref, mine_ref, other_ref, total_ref):
        high = place_ref[2]
        for ref, at in ((mine_ref, high), (other_ref, 1 - high)):
            ref[...] = (add(held_ref[at], a_ref[at]) + add(b_ref[at], c_ref[at])).astype(ref.dtype)
        total_ref[...] = add(acc_ref[...], term_ref[...]).astype(jnp.bfloat16)

    out_shape = [wide(rows, width), low(rows, width), low(*acc.shape)]
    return call(body, "fold", out_shape, [], place, held, *by, acc, term)


def join(place, mine, theirs):
    def body(place_ref, mine_ref, theirs_ref, out_ref):
        out_ref[place_ref[0]] = mine_ref[...]
        out_ref[1 - place_ref[0]] = theirs_ref[...]

    return call(body, "join", wide(2, *mine.shape), [], place, mine, theirs)


def permute(x, axis, to):
    n = lax.axis_size(axis)
    return lax.ppermute(x, axis, [(i, to(i)) for i in range(n) if 0 <= to(i) < n])


def exchange(x, axes):
    return lax.all_to_all(x, axes, split_axis=0, concat_axis=0, tiled=True)


def shards(queries, cotangent, encoded, kv_weight, neighbour_ids):
    q, g, enc = queries[0], cotangent[0], encoded[0]
    units, piece, enc_width = enc.shape
    groups = lax.axis_size("nbr")
    ctx = lax.axis_index("ctx")
    dp = lax.axis_index("dp")
    nbr = lax.axis_index("nbr")
    place = jnp.stack((ctx % 2, dp % 4, dp // 4)).astype(jnp.int32)

    copies = jnp.broadcast_to(enc[:, None], (units, groups, piece, enc_width))
    x = exchange(copies.reshape(units * groups, piece, enc_width), ("ctx", "nbr")).reshape(units * PART, enc_width)

    head = jnp.concatenate((q[:SPAN], g[:SPAN]), axis=1)
    ahead = permute(head, "ctx", lambda i: i - 1)

    unit_of = (neighbour_ids[0] // units).reshape(-1)
    scalars = jnp.concatenate((unit_of, nbr[None])).astype(jnp.int32)
    att, dq, grad, *partials = block(groups, scalars, q, g, ahead, kv_weight, x)

    terms = [permute(partials[k], "nbr", lambda i, k=k: (i + k) % groups) for k in range(1, groups)]

    sent, kept = products(place, x, grad)
    away = permute(sent, "ctx", lambda i: i ^ 1)
    tail = jnp.concatenate((att[:SPAN], dq[:SPAN]), axis=1)
    behind = permute(tail, "ctx", lambda i: i + 1)
    own, *sends, attended, query_grad = cut(place, kept, away, att, dq, behind)
    parts = [permute(sends[k - 1], "dp", lambda i, k=k: i // 4 * 4 + (i + k) % 4) for k in (1, 2, 3)]
    held, acc = x_sum(place, own, parts, partials[0], terms[1])
    held, acc = y_pair(place, held, permute(held, "ctx", lambda i: i ^ 2), acc, terms[0])
    by = [permute(held, "ctx", lambda i, b=b: i ^ b) for b in (4, 8, 12)]
    mine, other, total = fold(place, held, by, acc, terms[2])
    encoded_grad = exchange(total.reshape(units, piece, enc_width), "ctx")
    mine = add(mine, permute(other, "dp", lambda i: (i + 4) % 8))
    weight_grad = join(place, mine, permute(mine, "ctx", lambda i: i ^ 1))
    return (attended[None], query_grad[None], encoded_grad[None], weight_grad)


def add(a, b):
    return a.astype(jnp.float32) + b.astype(jnp.float32)


def solution(mesh):
    return jax.shard_map(
        shards,
        mesh=mesh,
        in_specs=(
            P("dp", "ctx", "nbr"),
            P("dp", "ctx", "nbr"),
            P("dp", "ctx", "nbr", None),
            P(None, None, "nbr"),
            P("dp", "ctx", None),
        ),
        out_specs=(
            P("dp", "ctx", "nbr"),
            P("dp", "ctx", "nbr"),
            P("dp", "ctx", "nbr", None),
            P(None, "dp", "nbr"),
        ),
        check_vma=False,
    )
```

```python
import math

import jax
import jax.numpy as jnp
from jax import lax
from jax.experimental import pallas as pl
from jax.experimental.pallas import tpu as pltpu
from jax.sharding import PartitionSpec as P

HEAD_DIM = 128
SPAN = 64
PART = 64
LEAD = SPAN - 1
SCALE = 1.0 / math.sqrt(HEAD_DIM)
NT = (((1,), (1,)), ((), ()))
TN = (((0,), (0,)), ((), ()))
NN = (((1,), (0,)), ((), ()))
VMEM = pl.BlockSpec(memory_space=pltpu.VMEM)
SMEM = pl.BlockSpec(memory_space=pltpu.SMEM)
PARAMS = pltpu.CompilerParams(vmem_limit_bytes=50 * 1024 * 1024)


def dot(a, b, dims):
    return lax.dot_general(a, b, dims, preferred_element_type=jnp.float32)


def span_rows(own, ahead):
    own, ahead = own.astype(jnp.float32), ahead.astype(jnp.float32)
    row = lax.broadcasted_iota(jnp.int32, ahead.shape, 0)
    mixed = jnp.concatenate((jnp.where(row < LEAD, ahead, own[:SPAN]), own[SPAN:]), axis=0)
    return pltpu.roll(mixed, own.shape[0] - LEAD, 0).astype(jnp.bfloat16)


def block_body(
    units_ref, q_ref, g_ref, ahead_ref, w_ref, x_ref, att_ref, dq_ref, grad, partial_ref, key, value, q_rows, g_rows, att, dq
):
    tokens, width = q_ref.shape
    all_rows = x_ref.shape[0]
    heads = width // HEAD_DIM
    chunk = 4 * PART
    for c in range(all_rows // chunk):
        rows = pl.ds(c * chunk, chunk)
        for kind, out in enumerate((key, value)):
            out[rows, :] = dot(x_ref[rows, :], w_ref[kind], NN).astype(jnp.bfloat16)
    for h in range(heads):
        cols = pl.ds(h * HEAD_DIM, HEAD_DIM)
        q_rows[:, cols] = span_rows(q_ref[:, cols], ahead_ref[:, cols])
        g_rows[:, cols] = span_rows(g_ref[:, cols], ahead_ref[:, pl.ds(width + h * HEAD_DIM, HEAD_DIM)])
    for j in range(tokens // SPAN):
        starts = [pl.multiple_of(units_ref[j * 4 + r] * PART, PART) for r in range(4)]
        rows = pl.ds(j * SPAN, SPAN)
        for h in range(heads):
            cols = pl.ds(h * HEAD_DIM, HEAD_DIM)
            q = q_rows[rows, cols]
            g = g_rows[rows, cols]
            k = jnp.concatenate([key[pl.ds(s, PART), cols] for s in starts], axis=0)
            v = jnp.concatenate([value[pl.ds(s, PART), cols] for s in starts], axis=0)
            scores = dot(q, k, NT) * SCALE
            raised = jnp.exp(scores - jnp.max(scores, axis=-1, keepdims=True))
            weights = raised / jnp.sum(raised, axis=-1, keepdims=True)
            low = weights.astype(jnp.bfloat16)
            d_weights = dot(g, v, NT)
            inner = jnp.sum(weights * d_weights, axis=-1, keepdims=True)
            d_scores = (weights * (d_weights - inner) * SCALE).astype(jnp.bfloat16)
            att[rows, cols] = dot(low, v, NN)
            dq[rows, cols] = dot(d_scores, k, NN)
            dk = dot(d_scores, q, TN).astype(jnp.bfloat16)
            dv = dot(low, g, TN).astype(jnp.bfloat16)
            for r, s in enumerate(starts):
                grad[0, pl.ds(s, PART), cols] = dk[r * PART : (r + 1) * PART]
                grad[1, pl.ds(s, PART), cols] = dv[r * PART : (r + 1) * PART]
    for h in range(heads):
        cols = pl.ds(h * HEAD_DIM, HEAD_DIM)
        att_ref[:, cols] = pltpu.roll(att[:, cols], LEAD, 0).astype(jnp.bfloat16)
        dq_ref[:, cols] = pltpu.roll(dq[:, cols], LEAD, 0).astype(jnp.bfloat16)
    for c in range(all_rows // chunk):
        rows = pl.ds(c * chunk, chunk)
        term = dot(grad[0, rows, :], w_ref[0], NT) + dot(grad[1, rows, :], w_ref[1], NT)
        partial_ref[rows, :] = term.astype(jnp.bfloat16)


def low(*shape):
    return jax.ShapeDtypeStruct(shape, jnp.bfloat16)


def wide(*shape):
    return jax.ShapeDtypeStruct(shape, jnp.float32)


def call(body, name, out_shape, scratch, place, *args):
    return pl.pallas_call(
        body,
        out_shape=out_shape,
        in_specs=[SMEM] + [VMEM] * len(args),
        out_specs=jax.tree.map(lambda _: VMEM, out_shape),
        scratch_shapes=scratch,
        compiler_params=PARAMS,
        name=name,
    )(place, *args)


def block(units_of, q, g, ahead, w, x):
    tokens, width = q.shape
    all_rows, enc_width = x.shape
    out_shape = [low(tokens, width), low(tokens, width), low(2, all_rows, width), low(all_rows, enc_width)]
    scratch = [pltpu.VMEM((all_rows, width), jnp.bfloat16)] * 2
    scratch += [pltpu.VMEM((tokens, width), jnp.bfloat16)] * 2
    scratch += [pltpu.VMEM((tokens, width), jnp.float32)] * 2
    return call(block_body, "block", out_shape, scratch, units_of, q, g, ahead, w, x)


def products(place, x, grad):
    enc_width, width = x.shape[1], grad.shape[2]

    def body(place_ref, x_ref, grad_ref, sent_ref, kept_ref):
        core = place_ref[0]
        for e in range(0, enc_width, 128):
            part = x_ref[:, e : e + 128].T
            sent_ref[e : e + 128, :] = dot(part, grad_ref[1 - core], NN).astype(jnp.bfloat16)
            kept_ref[e : e + 128, :] = dot(part, grad_ref[core], NN)

    return call(body, "products", [low(enc_width, width), wide(enc_width, width)], [], place, x, grad)


def cut(place, kept, away):
    enc_width, width = kept.shape
    rows = enc_width // 8

    def body(place_ref, kept_ref, away_ref, own_ref, *send_refs):
        x = place_ref[1]
        for high in range(2):
            for k in range(4):
                at = pl.multiple_of((high * 4 + lax.rem(x + k, 4)) * rows, 16)
                term = add(kept_ref[pl.ds(at, rows), :], away_ref[pl.ds(at, rows), :])
                if k:
                    send_refs[k - 1][high] = term.astype(jnp.bfloat16)
                else:
                    own_ref[high] = term

    return call(body, "cut", [wide(2, rows, width)] + [low(2, rows, width)] * 3, [], place, kept, away)


def y_pair(place, held, came, terms, att, dq, behind):
    units, groups, piece, enc_width = terms.shape
    width = att.shape[1]

    def body(_, held_ref, came_ref, terms_ref, att_ref, dq_ref, behind_ref, both_ref, total_ref, *full_refs):
        both_ref[...] = add(held_ref[...], came_ref[...]).astype(jnp.bfloat16)
        for u in range(units):
            total = add(terms_ref[u, 0], terms_ref[u, 1])
            for n in range(2, groups):
                total = add(total, terms_ref[u, n])
            total_ref[u] = total.astype(jnp.bfloat16)
        lead = lax.broadcasted_iota(jnp.int32, (SPAN, width), 0) < LEAD
        for n, (ref, full) in enumerate(zip((att_ref, dq_ref), full_refs)):
            came = behind_ref[:, n * width : (n + 1) * width].astype(jnp.float32)
            full[:SPAN, :] = jnp.where(lead, came, ref[:SPAN, :].astype(jnp.float32)).astype(jnp.bfloat16)
            full[SPAN:, :] = ref[SPAN:, :]

    out_shape = [low(*held.shape), low(units, piece, enc_width), low(*att.shape), low(*dq.shape)]
    return call(body, "y_pair", out_shape, [], place, held, came, terms, att, dq, behind)


def join(place, mine, theirs):
    def body(place_ref, mine_ref, theirs_ref, out_ref):
        out_ref[place_ref[0]] = mine_ref[...]
        out_ref[1 - place_ref[0]] = theirs_ref[...]

    return call(body, "join", wide(2, *mine.shape), [], place, mine, theirs)


def permute(x, axis, to):
    n = lax.axis_size(axis)
    return lax.ppermute(x, axis, [(i, to(i)) for i in range(n) if 0 <= to(i) < n])


def exchange(x):
    outer, inner, *rest = x.shape
    x = lax.all_to_all(x.reshape(outer * inner, *rest), ("ctx", "nbr"), split_axis=0, concat_axis=0, tiled=True)
    return x.reshape(outer, inner, *rest)


def shards(queries, cotangent, encoded, kv_weight, neighbour_ids):
    q, g, enc = queries[0], cotangent[0], encoded[0]
    units, piece, enc_width = enc.shape
    groups = lax.axis_size("nbr")
    ctx = lax.axis_index("ctx")
    dp = lax.axis_index("dp")
    place = jnp.stack((ctx % 2, dp % 4, dp // 4)).astype(jnp.int32)

    copies = jnp.broadcast_to(enc[:, None], (units, groups, piece, enc_width))
    x = exchange(copies).reshape(units * PART, enc_width)

    head = jnp.concatenate((q[:SPAN], g[:SPAN]), axis=1)
    ahead = permute(head, "ctx", lambda i: i - 1)

    unit_of = (neighbour_ids[0] // units).reshape(-1)
    att, dq, grad, partial = block(unit_of, q, g, ahead, kv_weight, x)

    terms = exchange(partial.reshape(units, groups, piece, enc_width))
    tail = jnp.concatenate((att[:SPAN], dq[:SPAN]), axis=1)
    behind = permute(tail, "ctx", lambda i: i + 1)

    sent, kept = products(place, x, grad)
    held, *sends = cut(place, kept, permute(sent, "ctx", lambda i: i ^ 1))
    for k in (1, 3, 2):
        held = add(held, permute(sends[k - 1], "dp", lambda i, k=k: i // 4 * 4 + (i + k) % 4))
    high = dp // 4
    other = lax.dynamic_index_in_dim(held, 1 - high, 0, keepdims=False).astype(jnp.bfloat16)
    mine = lax.dynamic_index_in_dim(held, high, 0, keepdims=False)
    rows = add(mine, permute(other, "dp", lambda i: (i + 4) % 8)).astype(jnp.bfloat16)
    came = permute(rows, "ctx", lambda i: i ^ 2)
    rows, encoded_grad, attended, query_grad = y_pair(place, rows, came, terms, att, dq, behind)
    by = [permute(rows, "ctx", lambda i, b=b: i ^ b) for b in (4, 8, 12)]
    mine = add(rows, by[0]) + add(by[1], by[2])
    weight_grad = join(place, mine, permute(mine, "ctx", lambda i: i ^ 1))
    return (attended[None], query_grad[None], encoded_grad[None], weight_grad)


def add(a, b):
    return a.astype(jnp.float32) + b.astype(jnp.float32)


def solution(mesh):
    return jax.shard_map(
        shards,
        mesh=mesh,
        in_specs=(
            P("dp", "ctx", "nbr"),
            P("dp", "ctx", "nbr"),
            P("dp", "ctx", "nbr", None),
            P(None, None, "nbr"),
            P("dp", "ctx", None),
        ),
        out_specs=(
            P("dp", "ctx", "nbr"),
            P("dp", "ctx", "nbr"),
            P("dp", "ctx", "nbr", None),
            P(None, "dp", "nbr"),
        ),
        check_vma=False,
    )
```

```python
import math

import jax
import jax.numpy as jnp
from jax import lax
from jax.experimental import pallas as pl
from jax.experimental.pallas import tpu as pltpu
from jax.sharding import PartitionSpec as P

HEAD_DIM = 128
SPAN = 64
PART = 64
LEAD = SPAN - 1
SCALE = 1.0 / math.sqrt(HEAD_DIM)
NT = (((1,), (1,)), ((), ()))
TN = (((0,), (0,)), ((), ()))
NN = (((1,), (0,)), ((), ()))
VMEM = pl.BlockSpec(memory_space=pltpu.VMEM)
SMEM = pl.BlockSpec(memory_space=pltpu.SMEM)
HBM = pl.BlockSpec(memory_space=pl.ANY)
PARAMS = pltpu.CompilerParams(vmem_limit_bytes=50 * 1024 * 1024)


def dot(a, b, dims):
    return lax.dot_general(a, b, dims, preferred_element_type=jnp.float32)


def span_rows(own, ahead):
    own, ahead = own.astype(jnp.float32), ahead.astype(jnp.float32)
    row = lax.broadcasted_iota(jnp.int32, ahead.shape, 0)
    mixed = jnp.concatenate((jnp.where(row < LEAD, ahead, own[:SPAN]), own[SPAN:]), axis=0)
    return pltpu.roll(mixed, own.shape[0] - LEAD, 0).astype(jnp.bfloat16)


def block_body(
    units_ref, q_ref, g_ref, ahead_ref, w_ref, x_hbm, att_ref, dq_ref, tail_ref, grad_hbm, partial_hbm,
    x, key, value, grad, partial, q_rows, g_rows, att, dq, x_sems, grad_sems, partial_sems,
):
    tokens, width = q_ref.shape
    heads = width // HEAD_DIM
    chunk = 4 * PART
    chunks = [pl.ds(c * chunk, chunk) for c in range(x.shape[0] // chunk)]
    head_cols = [pl.ds(h * HEAD_DIM, HEAD_DIM) for h in range(heads)]
    x_copies = [pltpu.make_async_copy(x_hbm.at[rows], x.at[rows], x_sems.at[c]) for c, rows in enumerate(chunks)]
    for copy in x_copies:
        copy.start()
    for h, cols in enumerate(head_cols):
        q_rows[:, cols] = span_rows(q_ref[:, cols], ahead_ref[:, cols])
        g_rows[:, cols] = span_rows(g_ref[:, cols], ahead_ref[:, pl.ds(width + h * HEAD_DIM, HEAD_DIM)])
    for copy, rows in zip(x_copies, chunks):
        copy.wait()
        for kind, out in enumerate((key, value)):
            out[rows, :] = dot(x[rows, :], w_ref[kind], NN).astype(jnp.bfloat16)
    for j in range(tokens // SPAN):
        starts = [pl.multiple_of(units_ref[j * 4 + r] * PART, PART) for r in range(4)]
        rows = pl.ds(j * SPAN, SPAN)
        qs = [q_rows[rows, cols] for cols in head_cols]
        gs = [g_rows[rows, cols] for cols in head_cols]
        ks = [jnp.concatenate([key[pl.ds(s, PART), cols] for s in starts], axis=0) for cols in head_cols]
        vs = [jnp.concatenate([value[pl.ds(s, PART), cols] for s in starts], axis=0) for cols in head_cols]
        scores = [dot(q, k, NT) * SCALE for q, k in zip(qs, ks)]
        d_weights = [dot(g, v, NT) for g, v in zip(gs, vs)]
        lows, d_scores = [], []
        for s, dw in zip(scores, d_weights):
            raised = jnp.exp(s - jnp.max(s, axis=-1, keepdims=True))
            weights = raised * (1.0 / jnp.sum(raised, axis=-1, keepdims=True))
            inner = jnp.sum(weights * dw, axis=-1, keepdims=True)
            lows.append(weights.astype(jnp.bfloat16))
            d_scores.append((weights * (dw - inner) * SCALE).astype(jnp.bfloat16))
        for h, cols in enumerate(head_cols):
            att[rows, cols] = dot(lows[h], vs[h], NN)
            dq[rows, cols] = dot(d_scores[h], ks[h], NN)
            dk = dot(d_scores[h], qs[h], TN).astype(jnp.bfloat16)
            dv = dot(lows[h], gs[h], TN).astype(jnp.bfloat16)
            for r, s in enumerate(starts):
                grad[0, pl.ds(s, PART), cols] = dk[r * PART : (r + 1) * PART]
                grad[1, pl.ds(s, PART), cols] = dv[r * PART : (r + 1) * PART]
    grad_copies = [pltpu.make_async_copy(grad.at[n], grad_hbm.at[n], grad_sems.at[n]) for n in range(2)]
    partial_copies = [
        pltpu.make_async_copy(partial.at[rows], partial_hbm.at[rows], partial_sems.at[c]) for c, rows in enumerate(chunks)
    ]
    for copy in grad_copies:
        copy.start()
    for copy, rows in zip(partial_copies, chunks):
        term = dot(grad[0, rows, :], w_ref[0], NT) + dot(grad[1, rows, :], w_ref[1], NT)
        partial[rows, :] = term.astype(jnp.bfloat16)
        copy.start()
    for cols in head_cols:
        att_ref[:, cols] = pltpu.roll(att[:, cols], LEAD, 0).astype(jnp.bfloat16)
        dq_ref[:, cols] = pltpu.roll(dq[:, cols], LEAD, 0).astype(jnp.bfloat16)
    tail_ref[:, :width] = att_ref[:SPAN, :]
    tail_ref[:, width:] = dq_ref[:SPAN, :]
    for copy in grad_copies + partial_copies:
        copy.wait()


def low(*shape):
    return jax.ShapeDtypeStruct(shape, jnp.bfloat16)


def wide(*shape):
    return jax.ShapeDtypeStruct(shape, jnp.float32)


def call(body, name, out_shape, scratch, place, *args):
    return pl.pallas_call(
        body,
        out_shape=out_shape,
        in_specs=[SMEM] + [VMEM] * len(args),
        out_specs=jax.tree.map(lambda _: VMEM, out_shape),
        scratch_shapes=scratch,
        compiler_params=PARAMS,
        name=name,
    )(place, *args)


def block(units_of, q, g, ahead, w, x):
    tokens, width = q.shape
    all_rows, enc_width = x.shape
    return pl.pallas_call(
        block_body,
        out_shape=[low(tokens, width), low(tokens, width), low(SPAN, 2 * width), low(2, all_rows, width), low(all_rows, enc_width)],
        in_specs=[SMEM] + [VMEM] * 4 + [HBM],
        out_specs=[VMEM] * 3 + [HBM] * 2,
        scratch_shapes=[pltpu.VMEM((all_rows, enc_width), jnp.bfloat16)]
        + [pltpu.VMEM((all_rows, width), jnp.bfloat16)] * 2
        + [pltpu.VMEM((2, all_rows, width), jnp.bfloat16), pltpu.VMEM((all_rows, enc_width), jnp.bfloat16)]
        + [pltpu.VMEM((tokens, width), jnp.bfloat16)] * 2
        + [pltpu.VMEM((tokens, width), jnp.float32)] * 2
        + [pltpu.SemaphoreType.DMA((4,)), pltpu.SemaphoreType.DMA((2,)), pltpu.SemaphoreType.DMA((4,))],
        compiler_params=PARAMS,
        name="block",
    )(units_of, q, g, ahead, w, x)


def products(place, x, grad):
    enc_width, width = x.shape[1], grad.shape[2]

    def body(place_ref, x_ref, grad_ref, sent_ref, kept_ref):
        core = place_ref[0]
        for e in range(0, enc_width, 128):
            part = x_ref[:, e : e + 128].T
            sent_ref[e : e + 128, :] = dot(part, grad_ref[1 - core], NN).astype(jnp.bfloat16)
            kept_ref[e : e + 128, :] = dot(part, grad_ref[core], NN)

    return call(body, "products", [low(enc_width, width), wide(enc_width, width)], [], place, x, grad)


def cut(place, kept, away):
    enc_width, width = kept.shape
    rows = enc_width // 8

    def body(place_ref, kept_ref, away_ref, own_ref, *send_refs):
        x = place_ref[1]
        for high in range(2):
            for k in range(4):
                at = pl.multiple_of((high * 4 + lax.rem(x + k, 4)) * rows, 16)
                term = add(kept_ref[pl.ds(at, rows), :], away_ref[pl.ds(at, rows), :])
                if k:
                    send_refs[k - 1][high] = term.astype(jnp.bfloat16)
                else:
                    own_ref[high] = term

    return call(body, "cut", [wide(2, rows, width)] + [low(2, rows, width)] * 3, [], place, kept, away)


def spread(x, groups):
    units, piece, enc_width = x.shape

    def body(x_ref, out_hbm, sems):
        copies = [pltpu.make_async_copy(x_ref, out_hbm.at[:, n], sems.at[n]) for n in range(groups)]
        for copy in copies:
            copy.start()
        for copy in copies:
            copy.wait()

    return pl.pallas_call(
        body,
        out_shape=low(units, groups, piece, enc_width),
        in_specs=[VMEM],
        out_specs=HBM,
        scratch_shapes=[pltpu.SemaphoreType.DMA((groups,))],
        compiler_params=PARAMS,
        name="spread",
    )(x)


def gather_up(place, terms, att, dq, behind):
    units, groups, piece, enc_width = terms.shape
    width = att.shape[1]

    def body(_, terms_ref, att_ref, dq_ref, behind_ref, total_ref, *full_refs):
        for u in range(units):
            total = add(terms_ref[u, 0], terms_ref[u, 1])
            for n in range(2, groups):
                total = add(total, terms_ref[u, n])
            total_ref[u] = total.astype(jnp.bfloat16)
        lead = lax.broadcasted_iota(jnp.int32, (SPAN, width), 0) < LEAD
        for n, (ref, full) in enumerate(zip((att_ref, dq_ref), full_refs)):
            came = behind_ref[:, n * width : (n + 1) * width].astype(jnp.float32)
            full[:SPAN, :] = jnp.where(lead, came, ref[:SPAN, :].astype(jnp.float32)).astype(jnp.bfloat16)
            full[SPAN:, :] = ref[SPAN:, :]

    out_shape = [low(units, piece, enc_width), low(*att.shape), low(*dq.shape)]
    return call(body, "gather_up", out_shape, [], place, terms, att, dq, behind)


def join(place, mine, theirs, after):
    def body(place_ref, mine_ref, theirs_ref, _, out_ref):
        out_ref[place_ref[0]] = mine_ref[...]
        out_ref[1 - place_ref[0]] = theirs_ref[...]

    return pl.pallas_call(
        body,
        out_shape=wide(2, *mine.shape),
        in_specs=[SMEM, VMEM, VMEM, HBM],
        out_specs=VMEM,
        compiler_params=PARAMS,
        name="join",
    )(place, mine, theirs, after)


def z_add(place, rows, came, after):
    def body(_, rows_ref, came_ref, __, out_ref):
        out_ref[...] = add(rows_ref[...], came_ref[...]).astype(jnp.bfloat16)

    return pl.pallas_call(
        body,
        out_shape=low(*rows.shape),
        in_specs=[SMEM, VMEM, VMEM, HBM],
        out_specs=VMEM,
        compiler_params=PARAMS,
        name="z_add",
    )(place, rows, came, after)


def permute(x, axis, to):
    n = lax.axis_size(axis)
    return lax.ppermute(x, axis, [(i, to(i)) for i in range(n) if 0 <= to(i) < n])


def exchange(x):
    outer, inner, *rest = x.shape
    x = lax.all_to_all(x.reshape(outer * inner, *rest), ("ctx", "nbr"), split_axis=0, concat_axis=0, tiled=True)
    return x.reshape(outer, inner, *rest)


def shards(queries, cotangent, encoded, kv_weight, neighbour_ids):
    q, g, enc = queries[0], cotangent[0], encoded[0]
    units, piece, enc_width = enc.shape
    groups = lax.axis_size("nbr")
    ctx = lax.axis_index("ctx")
    dp = lax.axis_index("dp")
    place = jnp.stack((ctx % 2, dp % 4, dp // 4)).astype(jnp.int32)

    x = exchange(spread(enc, groups)).reshape(units * PART, enc_width)

    head = jnp.concatenate((q[:SPAN], g[:SPAN]), axis=1)
    ahead = permute(head, "ctx", lambda i: i - 1)

    unit_of = (neighbour_ids[0] // units).reshape(-1)
    att, dq, tail, grad, partial = block(unit_of, q, g, ahead, kv_weight, x)

    terms = exchange(partial.reshape(units, groups, piece, enc_width))
    behind = permute(tail, "ctx", lambda i: i + 1)

    sent, kept = products(place, x, grad)
    held, *sends = cut(place, kept, permute(sent, "ctx", lambda i: i ^ 1))
    for k in (1, 3, 2):
        held = add(held, permute(sends[k - 1], "dp", lambda i, k=k: i // 4 * 4 + (i + k) % 4))
    high = dp // 4
    other = lax.dynamic_index_in_dim(held, 1 - high, 0, keepdims=False).astype(jnp.bfloat16)
    mine = lax.dynamic_index_in_dim(held, high, 0, keepdims=False)
    rows = z_add(place, mine, permute(other, "dp", lambda i: (i + 4) % 8), behind)
    for bit in (2, 4, 8):
        mine = add(rows, permute(rows, "ctx", lambda i, b=bit: i ^ b))
        rows = mine.astype(jnp.bfloat16)
    theirs = permute(mine, "ctx", lambda i: i ^ 1)
    encoded_grad, attended, query_grad = gather_up(place, terms, att, dq, behind)
    weight_grad = join(place, mine, theirs, encoded_grad)
    return (attended[None], query_grad[None], encoded_grad[None], weight_grad)


def add(a, b):
    return a.astype(jnp.float32) + b.astype(jnp.float32)


def solution(mesh):
    return jax.shard_map(
        shards,
        mesh=mesh,
        in_specs=(
            P("dp", "ctx", "nbr"),
            P("dp", "ctx", "nbr"),
            P("dp", "ctx", "nbr", None),
            P(None, None, "nbr"),
            P("dp", "ctx", None),
        ),
        out_specs=(
            P("dp", "ctx", "nbr"),
            P("dp", "ctx", "nbr"),
            P("dp", "ctx", "nbr", None),
            P(None, "dp", "nbr"),
        ),
        check_vma=False,
    )
```

```python
import math

import jax
import jax.numpy as jnp
from jax import lax
from jax.experimental import pallas as pl
from jax.experimental.pallas import tpu as pltpu
from jax.sharding import PartitionSpec as P

HEAD_DIM = 128
SPAN = 64
PART = 64
LEAD = SPAN - 1
SCALE = 1.0 / math.sqrt(HEAD_DIM)
NT = (((1,), (1,)), ((), ()))
TN = (((0,), (0,)), ((), ()))
NN = (((1,), (0,)), ((), ()))
VMEM = pl.BlockSpec(memory_space=pltpu.VMEM)
SMEM = pl.BlockSpec(memory_space=pltpu.SMEM)
HBM = pl.BlockSpec(memory_space=pltpu.HBM)
PARAMS = pltpu.CompilerParams(vmem_limit_bytes=50 * 1024 * 1024)


def dot(a, b, dims):
    return lax.dot_general(a, b, dims, preferred_element_type=jnp.float32)


def span_rows(own, ahead):
    own, ahead = own.astype(jnp.float32), ahead.astype(jnp.float32)
    row = lax.broadcasted_iota(jnp.int32, ahead.shape, 0)
    mixed = jnp.concatenate((jnp.where(row < LEAD, ahead, own[:SPAN]), own[SPAN:]), axis=0)
    return pltpu.roll(mixed, own.shape[0] - LEAD, 0).astype(jnp.bfloat16)


def block_body(
    units_ref, q_ref, g_ref, ahead_ref, w_ref, x_hbm, att_ref, dq_ref, tail_ref, grad_hbm, partial_hbm,
    x, key, value, grad, partial, q_rows, g_rows, att, dq, x_sems, grad_sems, partial_sems,
):
    tokens, width = q_ref.shape
    heads = width // HEAD_DIM
    chunk = 4 * PART
    chunks = [pl.ds(c * chunk, chunk) for c in range(x.shape[0] // chunk)]
    head_cols = [pl.ds(h * HEAD_DIM, HEAD_DIM) for h in range(heads)]
    x_copies = [pltpu.make_async_copy(x_hbm.at[rows], x.at[rows], x_sems.at[c]) for c, rows in enumerate(chunks)]
    for copy in x_copies:
        copy.start()
    for h, cols in enumerate(head_cols):
        q_rows[:, cols] = span_rows(q_ref[:, cols], ahead_ref[:, cols])
        g_rows[:, cols] = span_rows(g_ref[:, cols], ahead_ref[:, pl.ds(width + h * HEAD_DIM, HEAD_DIM)])
    for copy, rows in zip(x_copies, chunks):
        copy.wait()
        for kind, out in enumerate((key, value)):
            out[rows, :] = dot(x[rows, :], w_ref[kind], NN).astype(jnp.bfloat16)
    for j in range(tokens // SPAN):
        starts = [pl.multiple_of(units_ref[j * 4 + r] * PART, PART) for r in range(4)]
        rows = pl.ds(j * SPAN, SPAN)
        qs = [q_rows[rows, cols] for cols in head_cols]
        gs = [g_rows[rows, cols] for cols in head_cols]
        ks = [jnp.concatenate([key[pl.ds(s, PART), cols] for s in starts], axis=0) for cols in head_cols]
        vs = [jnp.concatenate([value[pl.ds(s, PART), cols] for s in starts], axis=0) for cols in head_cols]
        scores = [dot(q, k, NT) * SCALE for q, k in zip(qs, ks)]
        d_weights = [dot(g, v, NT) for g, v in zip(gs, vs)]
        lows, d_scores = [], []
        for s, dw in zip(scores, d_weights):
            raised = jnp.exp(s - jnp.max(s, axis=-1, keepdims=True))
            weights = raised * (1.0 / jnp.sum(raised, axis=-1, keepdims=True))
            inner = jnp.sum(weights * dw, axis=-1, keepdims=True)
            lows.append(weights.astype(jnp.bfloat16))
            d_scores.append((weights * (dw - inner) * SCALE).astype(jnp.bfloat16))
        for h, cols in enumerate(head_cols):
            att[rows, cols] = dot(lows[h], vs[h], NN)
            dq[rows, cols] = dot(d_scores[h], ks[h], NN)
            dk = dot(d_scores[h], qs[h], TN).astype(jnp.bfloat16)
            dv = dot(lows[h], gs[h], TN).astype(jnp.bfloat16)
            for r, s in enumerate(starts):
                grad[0, pl.ds(s, PART), cols] = dk[r * PART : (r + 1) * PART]
                grad[1, pl.ds(s, PART), cols] = dv[r * PART : (r + 1) * PART]
    grad_copies = [pltpu.make_async_copy(grad.at[n], grad_hbm.at[n], grad_sems.at[n]) for n in range(2)]
    for copy in grad_copies:
        copy.start()
    partial_copies = []
    for c, rows in enumerate(chunks):
        term = dot(grad[0, rows, :], w_ref[0], NT) + dot(grad[1, rows, :], w_ref[1], NT)
        units = pl.ds(c * 4, 4)
        partial[units] = term.astype(jnp.bfloat16).reshape(4, *partial.shape[1:])
        for n in range(partial.shape[1]):
            copy = pltpu.make_async_copy(partial.at[units, n], partial_hbm.at[n, units], partial_sems.at[c, n])
            copy.start()
            partial_copies.append(copy)
    for cols in head_cols:
        att_ref[:, cols] = pltpu.roll(att[:, cols], LEAD, 0).astype(jnp.bfloat16)
        dq_ref[:, cols] = pltpu.roll(dq[:, cols], LEAD, 0).astype(jnp.bfloat16)
    tail_ref[:, :width] = att_ref[:SPAN, :]
    tail_ref[:, width:] = dq_ref[:SPAN, :]
    for copy in grad_copies + partial_copies:
        copy.wait()


def low(*shape):
    return jax.ShapeDtypeStruct(shape, jnp.bfloat16)


def wide(*shape):
    return jax.ShapeDtypeStruct(shape, jnp.float32)


def call(body, name, out_shape, scratch, place, *args):
    return pl.pallas_call(
        body,
        out_shape=out_shape,
        in_specs=[SMEM] + [VMEM] * len(args),
        out_specs=jax.tree.map(lambda _: VMEM, out_shape),
        scratch_shapes=scratch,
        compiler_params=PARAMS,
        name=name,
    )(place, *args)


def block(units_of, q, g, ahead, w, x, slices):
    tokens, width = q.shape
    all_rows, enc_width = x.shape
    units, piece = all_rows // PART, PART // slices
    return pl.pallas_call(
        block_body,
        out_shape=[low(tokens, width), low(tokens, width), low(SPAN, 2 * width), low(2, all_rows, width), low(slices, units, piece, enc_width)],
        in_specs=[SMEM] + [VMEM] * 4 + [HBM],
        out_specs=[VMEM] * 3 + [HBM] * 2,
        scratch_shapes=[pltpu.VMEM((all_rows, enc_width), jnp.bfloat16)]
        + [pltpu.VMEM((all_rows, width), jnp.bfloat16)] * 2
        + [pltpu.VMEM((2, all_rows, width), jnp.bfloat16), pltpu.VMEM((units, slices, piece, enc_width), jnp.bfloat16)]
        + [pltpu.VMEM((tokens, width), jnp.bfloat16)] * 2
        + [pltpu.VMEM((tokens, width), jnp.float32)] * 2
        + [pltpu.SemaphoreType.DMA((4,)), pltpu.SemaphoreType.DMA((2,)), pltpu.SemaphoreType.DMA((units // 4, slices))],
        compiler_params=PARAMS,
        name="block",
    )(units_of, q, g, ahead, w, x)


def products(place, x, grad):
    enc_width, width = x.shape[1], grad.shape[2]

    def body(place_ref, x_hbm, grad_hbm, sent_ref, kept_ref, x_ref, grad_ref, sems):
        core = place_ref[0]
        copies = [
            pltpu.make_async_copy(x_hbm, x_ref, sems.at[0]),
            pltpu.make_async_copy(grad_hbm.at[1 - core], grad_ref.at[0], sems.at[1]),
            pltpu.make_async_copy(grad_hbm.at[core], grad_ref.at[1], sems.at[2]),
        ]
        for copy in copies:
            copy.start()
        for copy in copies:
            copy.wait()
        for e in range(0, enc_width, 128):
            part = x_ref[:, e : e + 128].T
            sent_ref[e : e + 128, :] = dot(part, grad_ref[0], NN).astype(jnp.bfloat16)
            kept_ref[e : e + 128, :] = dot(part, grad_ref[1], NN)

    return pl.pallas_call(
        body,
        out_shape=[low(enc_width, width), wide(enc_width, width)],
        in_specs=[SMEM, HBM, HBM],
        out_specs=[VMEM, VMEM],
        scratch_shapes=[
            pltpu.VMEM(x.shape, jnp.bfloat16),
            pltpu.VMEM(grad.shape, jnp.bfloat16),
            pltpu.SemaphoreType.DMA((3,)),
        ],
        compiler_params=PARAMS,
        name="products",
    )(place, x, grad)


def cut(place, kept, away, att, dq, behind):
    enc_width, width = kept.shape
    rows = enc_width // 8

    def body(place_ref, kept_ref, away_ref, att_ref, dq_ref, behind_ref, own_ref, *refs):
        send_refs, full_refs = refs[:3], refs[3:]
        x = place_ref[1]
        for high in range(2):
            for k in range(4):
                at = pl.multiple_of((high * 4 + lax.rem(x + k, 4)) * rows, 16)
                term = add(kept_ref[pl.ds(at, rows), :], away_ref[pl.ds(at, rows), :])
                if k:
                    send_refs[k - 1][high] = term.astype(jnp.bfloat16)
                else:
                    own_ref[high] = term
        lead = lax.broadcasted_iota(jnp.int32, (SPAN, width), 0) < LEAD
        for n, (ref, full) in enumerate(zip((att_ref, dq_ref), full_refs)):
            came = behind_ref[:, n * width : (n + 1) * width].astype(jnp.float32)
            full[:SPAN, :] = jnp.where(lead, came, ref[:SPAN, :].astype(jnp.float32)).astype(jnp.bfloat16)
            full[SPAN:, :] = ref[SPAN:, :]

    out_shape = [wide(2, rows, width)] + [low(2, rows, width)] * 3 + [low(*att.shape)] * 2
    return call(body, "cut", out_shape, [], place, kept, away, att, dq, behind)


def spread(x, groups):
    units, piece, enc_width = x.shape
    parts = [pl.ds(c, units // 4) for c in range(0, units, units // 4)]

    def body(x_hbm, out_hbm, held, in_sems, out_sems):
        ins = [pltpu.make_async_copy(x_hbm.at[part], held.at[part], in_sems.at[c]) for c, part in enumerate(parts)]
        for copy in ins:
            copy.start()
        outs = []
        for c, part in enumerate(parts):
            ins[c].wait()
            for n in range(groups):
                copy = pltpu.make_async_copy(held.at[part], out_hbm.at[part, n], out_sems.at[c, n])
                copy.start()
                outs.append(copy)
        for copy in outs:
            copy.wait()

    return pl.pallas_call(
        body,
        out_shape=low(units, groups, piece, enc_width),
        in_specs=[HBM],
        out_specs=HBM,
        scratch_shapes=[
            pltpu.VMEM(x.shape, jnp.bfloat16),
            pltpu.SemaphoreType.DMA((4,)),
            pltpu.SemaphoreType.DMA((4, groups)),
        ],
        compiler_params=PARAMS,
        name="spread",
    )(x)


def join(place, mine, theirs):
    def body(place_ref, mine_ref, theirs_ref, out_ref):
        out_ref[place_ref[0]] = mine_ref[...]
        out_ref[1 - place_ref[0]] = theirs_ref[...]

    return call(body, "join", wide(2, *mine.shape), [], place, mine, theirs)


def permute(x, axis, to):
    n = lax.axis_size(axis)
    return lax.ppermute(x, axis, [(i, to(i)) for i in range(n) if 0 <= to(i) < n])


def exchange(x):
    outer, inner, *rest = x.shape
    x = lax.all_to_all(x.reshape(outer * inner, *rest), ("ctx", "nbr"), split_axis=0, concat_axis=0, tiled=True)
    return x.reshape(outer, inner, *rest)


def shards(queries, cotangent, encoded, kv_weight, neighbour_ids):
    q, g, enc = queries[0], cotangent[0], encoded[0]
    units, piece, enc_width = enc.shape
    groups = lax.axis_size("nbr")
    ctx = lax.axis_index("ctx")
    dp = lax.axis_index("dp")
    place = jnp.stack((ctx % 2, dp % 4, dp // 4)).astype(jnp.int32)

    x = exchange(spread(enc, groups)).reshape(units * PART, enc_width)

    head = jnp.concatenate((q[:SPAN], g[:SPAN]), axis=1)
    ahead = permute(head, "ctx", lambda i: i - 1)

    unit_of = (neighbour_ids[0] // units).reshape(-1)
    att, dq, tail, grad, partial = block(unit_of, q, g, ahead, kv_weight, x, groups)
    behind = permute(tail, "ctx", lambda i: i + 1)

    total = lax.psum_scatter(partial, "nbr", scatter_dimension=0, tiled=False)
    encoded_grad = lax.all_to_all(total, "ctx", split_axis=0, concat_axis=0, tiled=True)

    sent, kept = products(place, x, grad)
    away = permute(sent, "ctx", lambda i: i ^ 1)
    held, *sends, attended, query_grad = cut(place, kept, away, att, dq, behind)
    for k in (1, 3, 2):
        held = add(held, permute(sends[k - 1], "dp", lambda i, k=k: i // 4 * 4 + (i + k) % 4))
    high = dp // 4
    other = lax.dynamic_index_in_dim(held, 1 - high, 0, keepdims=False).astype(jnp.bfloat16)
    mine = lax.dynamic_index_in_dim(held, high, 0, keepdims=False)
    mine = add(mine, permute(other, "dp", lambda i: (i + 4) % 8))
    for bit in (2, 4, 8):
        rows = mine.astype(jnp.bfloat16)
        mine = add(rows, permute(rows, "ctx", lambda i, b=bit: i ^ b))
    weight_grad = join(place, mine, permute(mine, "ctx", lambda i: i ^ 1))
    return (attended[None], query_grad[None], encoded_grad[None], weight_grad)


def add(a, b):
    return a.astype(jnp.float32) + b.astype(jnp.float32)


def solution(mesh):
    return jax.shard_map(
        shards,
        mesh=mesh,
        in_specs=(
            P("dp", "ctx", "nbr"),
            P("dp", "ctx", "nbr"),
            P("dp", "ctx", "nbr", None),
            P(None, None, "nbr"),
            P("dp", "ctx", None),
        ),
        out_specs=(
            P("dp", "ctx", "nbr"),
            P("dp", "ctx", "nbr"),
            P("dp", "ctx", "nbr", None),
            P(None, "dp", "nbr"),
        ),
        check_vma=False,
    )
```

```python
import math

import jax
import jax.numpy as jnp
from jax import lax
from jax.experimental import pallas as pl
from jax.experimental.pallas import tpu as pltpu
from jax.sharding import PartitionSpec as P

HEAD_DIM = 128
SPAN = 64
PART = 64
LEAD = SPAN - 1
SCALE = 1.0 / math.sqrt(HEAD_DIM)
NT = (((1,), (1,)), ((), ()))
TN = (((0,), (0,)), ((), ()))
NN = (((1,), (0,)), ((), ()))
VMEM = pl.BlockSpec(memory_space=pltpu.VMEM)
SMEM = pl.BlockSpec(memory_space=pltpu.SMEM)
HBM = pl.BlockSpec(memory_space=pltpu.HBM)
PARAMS = pltpu.CompilerParams(vmem_limit_bytes=28 * 1024 * 1024)


def dot(a, b, dims):
    return lax.dot_general(a, b, dims, preferred_element_type=jnp.float32)


def span_rows(own, ahead):
    own, ahead = own.astype(jnp.float32), ahead.astype(jnp.float32)
    row = lax.broadcasted_iota(jnp.int32, ahead.shape, 0)
    mixed = jnp.concatenate((jnp.where(row < LEAD, ahead, own[:SPAN]), own[SPAN:]), axis=0)
    return pltpu.roll(mixed, own.shape[0] - LEAD, 0).astype(jnp.bfloat16)


def block_body(
    units_ref, q_ref, g_ref, ahead_ref, w_ref, x, att_ref, dq_ref, tail_ref, sent_ref, kept_ref, *refs
):
    partial_hbms = refs[:-9]
    key, value, grad, partial, q_rows, g_rows, att, dq, partial_sems = refs[-9:]
    tokens, width = q_ref.shape
    heads = width // HEAD_DIM
    chunk = 4 * PART
    nbr, core = units_ref[units_ref.shape[0] - 2], units_ref[units_ref.shape[0] - 1]
    chunks = [pl.ds(c * chunk, chunk) for c in range(x.shape[0] // chunk)]
    head_cols = [pl.ds(h * HEAD_DIM, HEAD_DIM) for h in range(heads)]
    for h, cols in enumerate(head_cols):
        q_rows[:, cols] = span_rows(q_ref[:, cols], ahead_ref[:, cols])
        g_rows[:, cols] = span_rows(g_ref[:, cols], ahead_ref[:, pl.ds(width + h * HEAD_DIM, HEAD_DIM)])
    for rows in chunks:
        for kind, out in enumerate((key, value)):
            out[rows, :] = dot(x[rows, :], w_ref[kind], NN).astype(jnp.bfloat16)
    for j in range(tokens // SPAN):
        starts = [pl.multiple_of(units_ref[j * 4 + r] * PART, PART) for r in range(4)]
        rows = pl.ds(j * SPAN, SPAN)
        qs = [q_rows[rows, cols] for cols in head_cols]
        gs = [g_rows[rows, cols] for cols in head_cols]
        ks = [jnp.concatenate([key[pl.ds(s, PART), cols] for s in starts], axis=0) for cols in head_cols]
        vs = [jnp.concatenate([value[pl.ds(s, PART), cols] for s in starts], axis=0) for cols in head_cols]
        scores = [dot(q, k, NT) * SCALE for q, k in zip(qs, ks)]
        d_weights = [dot(g, v, NT) for g, v in zip(gs, vs)]
        lows, d_scores = [], []
        for s, dw in zip(scores, d_weights):
            raised = jnp.exp(s - jnp.max(s, axis=-1, keepdims=True))
            weights = raised * (1.0 / jnp.sum(raised, axis=-1, keepdims=True))
            inner = jnp.sum(weights * dw, axis=-1, keepdims=True)
            lows.append(weights.astype(jnp.bfloat16))
            d_scores.append((weights * (dw - inner) * SCALE).astype(jnp.bfloat16))
        for h, cols in enumerate(head_cols):
            att[rows, cols] = dot(lows[h], vs[h], NN)
            dq[rows, cols] = dot(d_scores[h], ks[h], NN)
            dk = dot(d_scores[h], qs[h], TN).astype(jnp.bfloat16)
            dv = dot(lows[h], gs[h], TN).astype(jnp.bfloat16)
            for r, s in enumerate(starts):
                grad[0, pl.ds(s, PART), cols] = dk[r * PART : (r + 1) * PART]
                grad[1, pl.ds(s, PART), cols] = dv[r * PART : (r + 1) * PART]
    partial_copies = []
    for c, rows in enumerate(chunks):
        term = dot(grad[0, rows, :], w_ref[0], NT) + dot(grad[1, rows, :], w_ref[1], NT)
        units = pl.ds(c * 4, 4)
        partial[units] = term.astype(jnp.bfloat16).reshape(4, *partial.shape[1:])
        for k, out in enumerate(partial_hbms):
            slice_of = lax.rem(nbr + k, len(partial_hbms))
            copy = pltpu.make_async_copy(partial.at[units, slice_of], out.at[units], partial_sems.at[c, k])
            copy.start()
            partial_copies.append(copy)
    for e in range(0, x.shape[1], 128):
        part = x[:, e : e + 128].T
        sent_ref[e : e + 128, :] = dot(part, grad[1 - core], NN).astype(jnp.bfloat16)
        kept_ref[e : e + 128, :] = dot(part, grad[core], NN)
    for cols in head_cols:
        att_ref[:, cols] = pltpu.roll(att[:, cols], LEAD, 0).astype(jnp.bfloat16)
        dq_ref[:, cols] = pltpu.roll(dq[:, cols], LEAD, 0).astype(jnp.bfloat16)
    tail_ref[:, :width] = att_ref[:SPAN, :]
    tail_ref[:, width:] = dq_ref[:SPAN, :]
    for copy in partial_copies:
        copy.wait()


def low(*shape):
    return jax.ShapeDtypeStruct(shape, jnp.bfloat16)


def wide(*shape):
    return jax.ShapeDtypeStruct(shape, jnp.float32)


def call(body, name, out_shape, scratch, place, *args):
    return pl.pallas_call(
        body,
        out_shape=out_shape,
        in_specs=[SMEM] + [VMEM] * len(args),
        out_specs=jax.tree.map(lambda _: VMEM, out_shape),
        scratch_shapes=scratch,
        compiler_params=PARAMS,
        name=name,
    )(place, *args)


def block(scalars, q, g, ahead, w, x, slices):
    tokens, width = q.shape
    all_rows, enc_width = x.shape
    units, piece = all_rows // PART, PART // slices
    return pl.pallas_call(
        block_body,
        out_shape=[low(tokens, width), low(tokens, width), low(SPAN, 2 * width)]
        + [low(enc_width, width), wide(enc_width, width)]
        + [low(units, piece, enc_width)] * slices,
        in_specs=[SMEM] + [VMEM] * 5,
        out_specs=[VMEM] * 5 + [HBM] * slices,
        scratch_shapes=[pltpu.VMEM((all_rows, width), jnp.bfloat16)] * 2
        + [pltpu.VMEM((2, all_rows, width), jnp.bfloat16), pltpu.VMEM((units, slices, piece, enc_width), jnp.bfloat16)]
        + [pltpu.VMEM((tokens, width), jnp.bfloat16)] * 2
        + [pltpu.VMEM((tokens, width), jnp.float32)] * 2
        + [pltpu.SemaphoreType.DMA((units // 4, slices))],
        compiler_params=PARAMS,
        name="block",
    )(scalars, q, g, ahead, w, x)


def cut(place, kept, away, att, dq, behind):
    enc_width, width = kept.shape
    rows = enc_width // 8

    def body(place_ref, kept_ref, away_ref, att_ref, dq_ref, behind_ref, own_ref, *refs):
        send_refs, full_refs = refs[:3], refs[3:]
        x = place_ref[1]
        for high in range(2):
            for k in range(4):
                at = pl.multiple_of((high * 4 + lax.rem(x + k, 4)) * rows, 16)
                term = add(kept_ref[pl.ds(at, rows), :], away_ref[pl.ds(at, rows), :])
                if k:
                    send_refs[k - 1][high] = term.astype(jnp.bfloat16)
                else:
                    own_ref[high] = term
        lead = lax.broadcasted_iota(jnp.int32, (SPAN, width), 0) < LEAD
        for n, (ref, full) in enumerate(zip((att_ref, dq_ref), full_refs)):
            came = behind_ref[:, n * width : (n + 1) * width].astype(jnp.float32)
            full[:SPAN, :] = jnp.where(lead, came, ref[:SPAN, :].astype(jnp.float32)).astype(jnp.bfloat16)
            full[SPAN:, :] = ref[SPAN:, :]

    out_shape = [wide(2, rows, width)] + [low(2, rows, width)] * 3 + [low(*att.shape)] * 2
    return call(body, "cut", out_shape, [], place, kept, away, att, dq, behind)


def spread(x, groups):
    units, piece, enc_width = x.shape
    parts = [pl.ds(c, units // 4) for c in range(0, units, units // 4)]

    def body(x_hbm, out_hbm, held, in_sems, out_sems):
        ins = [pltpu.make_async_copy(x_hbm.at[part], held.at[part], in_sems.at[c]) for c, part in enumerate(parts)]
        for copy in ins:
            copy.start()
        outs = []
        for c, part in enumerate(parts):
            ins[c].wait()
            for n in range(groups):
                copy = pltpu.make_async_copy(held.at[part], out_hbm.at[part, n], out_sems.at[c, n])
                copy.start()
                outs.append(copy)
        for copy in outs:
            copy.wait()

    return pl.pallas_call(
        body,
        out_shape=low(units, groups, piece, enc_width),
        in_specs=[HBM],
        out_specs=HBM,
        scratch_shapes=[
            pltpu.VMEM(x.shape, jnp.bfloat16),
            pltpu.SemaphoreType.DMA((4,)),
            pltpu.SemaphoreType.DMA((4, groups)),
        ],
        compiler_params=pltpu.CompilerParams(vmem_limit_bytes=56 * 1024 * 1024),
        name="spread",
    )(x)


def x_sum(place, own, parts, partial, term):
    _, rows, width = own.shape

    def body(place_ref, own_ref, *refs):
        part_refs, partial_ref, term_ref, mine_ref, other_ref, acc_ref = refs[:3], *refs[3:]
        high = place_ref[2]
        for ref, at in ((mine_ref, high), (other_ref, 1 - high)):
            total = own_ref[at]
            for part in part_refs:
                total = add(total, part[at])
            ref[...] = total.astype(ref.dtype)
        acc_ref[...] = add(partial_ref[...], term_ref[...])

    out_shape = [wide(rows, width), low(rows, width), wide(*partial.shape)]
    return call(body, "x_sum", out_shape, [], place, own, *parts, partial, term)


def z_sum(place, mine, came, *held):
    def body(_, mine_ref, came_ref, *refs):
        refs[len(held)][...] = add(mine_ref[...], came_ref[...]).astype(jnp.bfloat16)

    return pl.pallas_call(
        body,
        out_shape=[low(*mine.shape)] + [low(*h.shape) for h in held],
        in_specs=[SMEM, VMEM, VMEM] + [HBM] * len(held),
        out_specs=[VMEM] + [HBM] * len(held),
        input_output_aliases={3 + n: 1 + n for n in range(len(held))},
        compiler_params=PARAMS,
        name="z_sum",
    )(place, mine, came, *held)


def y_sum(place, rows, came, acc, term, last):
    def body(_, rows_ref, came_ref, acc_ref, term_ref, sum_ref, out_ref):
        sum_ref[...] = add(rows_ref[...], came_ref[...]).astype(sum_ref.dtype)
        out_ref[...] = add(acc_ref[...], term_ref[...]).astype(out_ref.dtype)

    kind = low if last else wide
    out_shape = [(wide if last else low)(*rows.shape), kind(*acc.shape)]
    return call(body, "y_last" if last else "y_sum", out_shape, [], place, rows, came, acc, term)


def join(place, mine, theirs):
    def body(place_ref, mine_ref, theirs_ref, out_ref):
        out_ref[place_ref[0]] = mine_ref[...]
        out_ref[1 - place_ref[0]] = theirs_ref[...]

    return call(body, "join", wide(2, *mine.shape), [], place, mine, theirs)


def permute(x, axis, to):
    n = lax.axis_size(axis)
    return lax.ppermute(x, axis, [(i, to(i)) for i in range(n) if 0 <= to(i) < n])


def exchange(x):
    outer, inner, *rest = x.shape
    x = lax.all_to_all(x.reshape(outer * inner, *rest), ("ctx", "nbr"), split_axis=0, concat_axis=0, tiled=True)
    return x.reshape(outer, inner, *rest)


def shards(queries, cotangent, encoded, kv_weight, neighbour_ids):
    q, g, enc = queries[0], cotangent[0], encoded[0]
    units, piece, enc_width = enc.shape
    groups = lax.axis_size("nbr")
    ctx = lax.axis_index("ctx")
    dp = lax.axis_index("dp")
    nbr = lax.axis_index("nbr")
    place = jnp.stack((ctx % 2, dp % 4, dp // 4)).astype(jnp.int32)

    x = exchange(spread(enc, groups)).reshape(units * PART, enc_width)

    head = jnp.concatenate((q[:SPAN], g[:SPAN]), axis=1)
    ahead = permute(head, "ctx", lambda i: i - 1)

    unit_of = (neighbour_ids[0] // units).reshape(-1)
    scalars = jnp.concatenate((unit_of, nbr[None], (ctx % 2)[None])).astype(jnp.int32)
    att, dq, tail, sent, kept, *partials = block(scalars, q, g, ahead, kv_weight, x, groups)

    def returned(x, k):
        return permute(x, "nbr", lambda i: (i + k) % groups)

    term = returned(partials[2], 2)
    behind = permute(tail, "ctx", lambda i: i + 1)
    away = permute(sent, "ctx", lambda i: i ^ 1)
    own, *sends, attended, query_grad = cut(place, kept, away, att, dq, behind)
    parts = [permute(sends[k - 1], "dp", lambda i, k=k: i // 4 * 4 + (i + k) % 4) for k in (1, 2, 3)]
    mine, other, acc = x_sum(place, own, parts, partials[0], term)
    rows, first, third = z_sum(place, mine, permute(other, "dp", lambda i: (i + 4) % 8), partials[1], partials[3])

    rows = add(rows, permute(rows, "ctx", lambda i: i ^ 2)).astype(jnp.bfloat16)
    rows, acc = y_sum(place, rows, permute(rows, "ctx", lambda i: i ^ 4), acc, returned(first, 1), False)
    mine, total = y_sum(place, rows, permute(rows, "ctx", lambda i: i ^ 8), acc, returned(third, 3), True)
    encoded_grad = lax.all_to_all(total, "ctx", split_axis=0, concat_axis=0, tiled=True)
    weight_grad = join(place, mine, permute(mine, "ctx", lambda i: i ^ 1))
    return (attended[None], query_grad[None], encoded_grad[None], weight_grad)


def add(a, b):
    return a.astype(jnp.float32) + b.astype(jnp.float32)


def solution(mesh):
    return jax.shard_map(
        shards,
        mesh=mesh,
        in_specs=(
            P("dp", "ctx", "nbr"),
            P("dp", "ctx", "nbr"),
            P("dp", "ctx", "nbr", None),
            P(None, None, "nbr"),
            P("dp", "ctx", None),
        ),
        out_specs=(
            P("dp", "ctx", "nbr"),
            P("dp", "ctx", "nbr"),
            P("dp", "ctx", "nbr", None),
            P(None, "dp", "nbr"),
        ),
        check_vma=False,
    )
```

```python
import math

import jax
import jax.numpy as jnp
from jax import lax
from jax.experimental import pallas as pl
from jax.experimental.pallas import tpu as pltpu
from jax.sharding import PartitionSpec as P

HEAD_DIM = 128
SPAN = 64
PART = 64
LEAD = SPAN - 1
SCALE = 1.0 / math.sqrt(HEAD_DIM)
NT = (((1,), (1,)), ((), ()))
TN = (((0,), (0,)), ((), ()))
NN = (((1,), (0,)), ((), ()))
VMEM = pl.BlockSpec(memory_space=pltpu.VMEM)
SMEM = pl.BlockSpec(memory_space=pltpu.SMEM)
HBM = pl.BlockSpec(memory_space=pltpu.HBM)
PARAMS = pltpu.CompilerParams(vmem_limit_bytes=50 * 1024 * 1024)


def dot(a, b, dims):
    return lax.dot_general(a, b, dims, preferred_element_type=jnp.float32)


def span_rows(own, ahead):
    own, ahead = own.astype(jnp.float32), ahead.astype(jnp.float32)
    row = lax.broadcasted_iota(jnp.int32, ahead.shape, 0)
    mixed = jnp.concatenate((jnp.where(row < LEAD, ahead, own[:SPAN]), own[SPAN:]), axis=0)
    return pltpu.roll(mixed, own.shape[0] - LEAD, 0).astype(jnp.bfloat16)


def block_body(
    units_ref, q_hbm, g_hbm, ahead_hbm, w_hbm, x, att_ref, dq_ref, tail_ref, sent_ref, kept_ref, partial_hbm,
    key, value, grad, partial, q_ref, g_ref, ahead_ref, w_ref, q_rows, g_rows, att, dq, in_sems, out_sems,
):
    pairs = ((w_hbm, w_ref), (q_hbm, q_ref), (g_hbm, g_ref), (ahead_hbm, ahead_ref))
    copies_in = [pltpu.make_async_copy(source, held, in_sems.at[n]) for n, (source, held) in enumerate(pairs)]
    for copy in copies_in:
        copy.start()
    tokens, width = q_ref.shape
    heads = width // HEAD_DIM
    chunk = 4 * PART
    core = units_ref[units_ref.shape[0] - 1]
    chunks = [pl.ds(c * chunk, chunk) for c in range(x.shape[0] // chunk)]
    head_cols = [pl.ds(h * HEAD_DIM, HEAD_DIM) for h in range(heads)]
    copies_in[0].wait()
    for rows in chunks:
        for kind, out in enumerate((key, value)):
            out[rows, :] = dot(x[rows, :], w_ref[kind], NN).astype(jnp.bfloat16)
    for copy in copies_in[1:]:
        copy.wait()
    for h, cols in enumerate(head_cols):
        q_rows[:, cols] = span_rows(q_ref[:, cols], ahead_ref[:, cols])
        g_rows[:, cols] = span_rows(g_ref[:, cols], ahead_ref[:, pl.ds(width + h * HEAD_DIM, HEAD_DIM)])
    for j in range(tokens // SPAN):
        starts = [pl.multiple_of(units_ref[j * 4 + r] * PART, PART) for r in range(4)]
        rows = pl.ds(j * SPAN, SPAN)
        qs = [q_rows[rows, cols] for cols in head_cols]
        gs = [g_rows[rows, cols] for cols in head_cols]
        ks = [jnp.concatenate([key[pl.ds(s, PART), cols] for s in starts], axis=0) for cols in head_cols]
        vs = [jnp.concatenate([value[pl.ds(s, PART), cols] for s in starts], axis=0) for cols in head_cols]
        scores = [dot(q, k, NT) * SCALE for q, k in zip(qs, ks)]
        d_weights = [dot(g, v, NT) for g, v in zip(gs, vs)]
        lows, d_scores = [], []
        for s, dw in zip(scores, d_weights):
            raised = jnp.exp(s - jnp.max(s, axis=-1, keepdims=True))
            weights = raised * (1.0 / jnp.sum(raised, axis=-1, keepdims=True))
            inner = jnp.sum(weights * dw, axis=-1, keepdims=True)
            lows.append(weights.astype(jnp.bfloat16))
            d_scores.append((weights * (dw - inner) * SCALE).astype(jnp.bfloat16))
        for h, cols in enumerate(head_cols):
            att[rows, cols] = dot(lows[h], vs[h], NN)
            dq[rows, cols] = dot(d_scores[h], ks[h], NN)
            dk = dot(d_scores[h], qs[h], TN).astype(jnp.bfloat16)
            dv = dot(lows[h], gs[h], TN).astype(jnp.bfloat16)
            for r, s in enumerate(starts):
                grad[0, pl.ds(s, PART), cols] = dk[r * PART : (r + 1) * PART]
                grad[1, pl.ds(s, PART), cols] = dv[r * PART : (r + 1) * PART]
    partial_copies = []
    for c, rows in enumerate(chunks):
        term = dot(grad[0, rows, :], w_ref[0], NT) + dot(grad[1, rows, :], w_ref[1], NT)
        partial[rows, :] = term.astype(jnp.bfloat16)
        copy = pltpu.make_async_copy(partial.at[rows], partial_hbm.at[rows], out_sems.at[c])
        copy.start()
        partial_copies.append(copy)
    for e in range(0, x.shape[1], 128):
        part = x[:, e : e + 128].T
        sent_ref[e : e + 128, :] = dot(part, grad[1 - core], NN).astype(jnp.bfloat16)
        kept_ref[e : e + 128, :] = dot(part, grad[core], NN)
    for cols in head_cols:
        att_ref[:, cols] = pltpu.roll(att[:, cols], LEAD, 0).astype(jnp.bfloat16)
        dq_ref[:, cols] = pltpu.roll(dq[:, cols], LEAD, 0).astype(jnp.bfloat16)
    tail_ref[:, :width] = att_ref[:SPAN, :]
    tail_ref[:, width:] = dq_ref[:SPAN, :]
    for copy in partial_copies:
        copy.wait()


def low(*shape):
    return jax.ShapeDtypeStruct(shape, jnp.bfloat16)


def wide(*shape):
    return jax.ShapeDtypeStruct(shape, jnp.float32)


def call(body, name, out_shape, scratch, place, *args):
    return pl.pallas_call(
        body,
        out_shape=out_shape,
        in_specs=[SMEM] + [VMEM] * len(args),
        out_specs=jax.tree.map(lambda _: VMEM, out_shape),
        scratch_shapes=scratch,
        compiler_params=PARAMS,
        name=name,
    )(place, *args)


def block(scalars, q, g, ahead, w, x):
    tokens, width = q.shape
    all_rows, enc_width = x.shape
    rows = pltpu.VMEM((all_rows, width), jnp.bfloat16)
    half = pltpu.VMEM((tokens, width), jnp.bfloat16)
    return pl.pallas_call(
        block_body,
        out_shape=[low(tokens, width), low(tokens, width), low(SPAN, 2 * width)]
        + [low(enc_width, width), wide(enc_width, width), low(all_rows, enc_width)],
        in_specs=[SMEM] + [HBM] * 4 + [VMEM],
        out_specs=[VMEM] * 5 + [HBM],
        scratch_shapes=[rows, rows, pltpu.VMEM((2, all_rows, width), jnp.bfloat16)]
        + [pltpu.VMEM((all_rows, enc_width), jnp.bfloat16), half, half]
        + [pltpu.VMEM(ahead.shape, jnp.bfloat16), pltpu.VMEM(w.shape, jnp.bfloat16), half, half]
        + [pltpu.VMEM((tokens, width), jnp.float32)] * 2
        + [pltpu.SemaphoreType.DMA((4,))] * 2,
        compiler_params=pltpu.CompilerParams(vmem_limit_bytes=52 * 1024 * 1024),
        name="block",
    )(scalars, q, g, ahead, w, x)


def cut(place, kept, away):
    enc_width, width = kept.shape
    rows = enc_width // 8

    def body(place_ref, kept_ref, away_ref, own_ref, *send_refs):
        x = place_ref[1]
        for high in range(2):
            for k in range(4):
                at = pl.multiple_of((high * 4 + lax.rem(x + k, 4)) * rows, 16)
                term = add(kept_ref[pl.ds(at, rows), :], away_ref[pl.ds(at, rows), :])
                if k:
                    send_refs[k - 1][high] = term.astype(jnp.bfloat16)
                else:
                    own_ref[high] = term

    return call(body, "cut", [wide(2, rows, width)] + [low(2, rows, width)] * 3, [], place, kept, away)


def spread(x, groups):
    units, piece, enc_width = x.shape
    parts = [pl.ds(c, units // 4) for c in range(0, units, units // 4)]

    def body(x_hbm, out_hbm, held, in_sems, out_sems):
        ins = [pltpu.make_async_copy(x_hbm.at[part], held.at[part], in_sems.at[c]) for c, part in enumerate(parts)]
        for copy in ins:
            copy.start()
        outs = []
        for c, part in enumerate(parts):
            ins[c].wait()
            for n in range(groups):
                copy = pltpu.make_async_copy(held.at[part], out_hbm.at[part, n], out_sems.at[c, n])
                copy.start()
                outs.append(copy)
        for copy in outs:
            copy.wait()

    return pl.pallas_call(
        body,
        out_shape=low(units, groups, piece, enc_width),
        in_specs=[HBM],
        out_specs=HBM,
        scratch_shapes=[
            pltpu.VMEM(x.shape, jnp.bfloat16),
            pltpu.SemaphoreType.DMA((4,)),
            pltpu.SemaphoreType.DMA((4, groups)),
        ],
        compiler_params=pltpu.CompilerParams(vmem_limit_bytes=56 * 1024 * 1024),
        name="spread",
    )(x)


def gather_up(place, terms, att, dq, behind):
    units, groups, piece, enc_width = terms.shape
    width = att.shape[1]

    def body(_, terms_ref, att_ref, dq_ref, behind_ref, total_ref, *full_refs):
        for u in range(units):
            total = add(terms_ref[u, 0], terms_ref[u, 1])
            for n in range(2, groups):
                total = add(total, terms_ref[u, n])
            total_ref[u] = total.astype(jnp.bfloat16)
        lead = lax.broadcasted_iota(jnp.int32, (SPAN, width), 0) < LEAD
        for n, (ref, full) in enumerate(zip((att_ref, dq_ref), full_refs)):
            came = behind_ref[:, n * width : (n + 1) * width].astype(jnp.float32)
            full[:SPAN, :] = jnp.where(lead, came, ref[:SPAN, :].astype(jnp.float32)).astype(jnp.bfloat16)
            full[SPAN:, :] = ref[SPAN:, :]

    out_shape = [low(units, piece, enc_width), low(*att.shape), low(*dq.shape)]
    return call(body, "gather_up", out_shape, [], place, terms, att, dq, behind)


def sum_rows(place, name, rows, *after):
    def body(_, *refs):
        terms = [ref[...] for ref in refs[: len(rows)]]
        while len(terms) > 1:
            terms = [add(a, b) for a, b in zip(terms[::2], terms[1::2])]
        refs[-1][...] = terms[0].astype(jnp.bfloat16)

    return pl.pallas_call(
        body,
        out_shape=low(*rows[0].shape),
        in_specs=[SMEM] + [VMEM] * len(rows) + [HBM] * len(after),
        out_specs=VMEM,
        compiler_params=PARAMS,
        name=name,
    )(place, *rows, *after)


def join(place, mine, theirs):
    def body(place_ref, mine_ref, theirs_ref, out_ref):
        out_ref[place_ref[0]] = mine_ref[...]
        out_ref[1 - place_ref[0]] = theirs_ref[...]

    return call(body, "join", wide(2, *mine.shape), [], place, mine, theirs)


def permute(x, axis, to):
    n = lax.axis_size(axis)
    return lax.ppermute(x, axis, [(i, to(i)) for i in range(n) if 0 <= to(i) < n])


def exchange(x):
    outer, inner, *rest = x.shape
    x = lax.all_to_all(x.reshape(outer * inner, *rest), ("ctx", "nbr"), split_axis=0, concat_axis=0, tiled=True)
    return x.reshape(outer, inner, *rest)


def shards(queries, cotangent, encoded, kv_weight, neighbour_ids):
    q, g, enc = queries[0], cotangent[0], encoded[0]
    units, piece, enc_width = enc.shape
    groups = lax.axis_size("nbr")
    ctx = lax.axis_index("ctx")
    dp = lax.axis_index("dp")
    place = jnp.stack((ctx % 2, dp % 4, dp // 4)).astype(jnp.int32)

    x = exchange(spread(enc, groups)).reshape(units * PART, enc_width)

    head = jnp.concatenate((q[:SPAN], g[:SPAN]), axis=1)
    ahead = permute(head, "ctx", lambda i: i - 1)

    unit_of = (neighbour_ids[0] // units).reshape(-1)
    scalars = jnp.concatenate((unit_of, (ctx % 2)[None])).astype(jnp.int32)
    att, dq, tail, sent, kept, partial = block(scalars, q, g, ahead, kv_weight, x)

    terms = exchange(partial.reshape(units, groups, piece, enc_width))
    behind = permute(tail, "ctx", lambda i: i + 1)

    held, *sends = cut(place, kept, permute(sent, "ctx", lambda i: i ^ 1))
    for k in (1, 3, 2):
        held = add(held, permute(sends[k - 1], "dp", lambda i, k=k: i // 4 * 4 + (i + k) % 4))
    high = dp // 4
    held = held.astype(jnp.bfloat16)
    other = lax.dynamic_index_in_dim(held, 1 - high, 0, keepdims=False)
    mine = lax.dynamic_index_in_dim(held, high, 0, keepdims=False)
    owners = lax.axis_size("ctx")
    quad = (
        mine,
        permute(other, "dp", lambda i: i ^ 4),
        permute(mine, "ctx", lambda i: i ^ 2),
        permute(other, ("dp", "ctx"), lambda i: i ^ (4 * owners + 2)),
    )
    rows = sum_rows(place, "z_and_y", quad, behind)
    encoded_grad, attended, query_grad = gather_up(place, terms, att, dq, behind)
    rows = sum_rows(place, "y", (rows, permute(rows, "ctx", lambda i: i ^ 4)), encoded_grad)
    mine = add(rows, permute(rows, "ctx", lambda i: i ^ 8))
    weight_grad = join(place, mine, permute(mine, "ctx", lambda i: i ^ 1))
    return (attended[None], query_grad[None], encoded_grad[None], weight_grad)


def add(a, b):
    return a.astype(jnp.float32) + b.astype(jnp.float32)


def solution(mesh):
    return jax.shard_map(
        shards,
        mesh=mesh,
        in_specs=(
            P("dp", "ctx", "nbr"),
            P("dp", "ctx", "nbr"),
            P("dp", "ctx", "nbr", None),
            P(None, None, "nbr"),
            P("dp", "ctx", None),
        ),
        out_specs=(
            P("dp", "ctx", "nbr"),
            P("dp", "ctx", "nbr"),
            P("dp", "ctx", "nbr", None),
            P(None, "dp", "nbr"),
        ),
        check_vma=False,
    )
```

```python
import math

import jax
import jax.numpy as jnp
from jax import lax
from jax.experimental import pallas as pl
from jax.experimental.pallas import tpu as pltpu
from jax.sharding import PartitionSpec as P

HEAD_DIM = 128
SPAN = 64
PART = 64
LEAD = SPAN - 1
SCALE = 1.0 / math.sqrt(HEAD_DIM)
NT = (((1,), (1,)), ((), ()))
TN = (((0,), (0,)), ((), ()))
NN = (((1,), (0,)), ((), ()))
VMEM = pl.BlockSpec(memory_space=pltpu.VMEM)
SMEM = pl.BlockSpec(memory_space=pltpu.SMEM)
HBM = pl.BlockSpec(memory_space=pltpu.HBM)
PARAMS = pltpu.CompilerParams(vmem_limit_bytes=50 * 1024 * 1024)


def dot(a, b, dims):
    return lax.dot_general(a, b, dims, preferred_element_type=jnp.float32)


def span_rows(own, ahead):
    own, ahead = own.astype(jnp.float32), ahead.astype(jnp.float32)
    row = lax.broadcasted_iota(jnp.int32, ahead.shape, 0)
    mixed = jnp.concatenate((jnp.where(row < LEAD, ahead, own[:SPAN]), own[SPAN:]), axis=0)
    return pltpu.roll(mixed, own.shape[0] - LEAD, 0).astype(jnp.bfloat16)


def block_body(
    units_ref, q_hbm, g_hbm, ahead_hbm, w_hbm, x, rows_ref, sent_hbm, kept_hbm, partial_hbm,
    key, value, grad, partial, sent, kept, q_ref, g_ref, ahead_ref, w_ref, q_rows, g_rows, att, dq, in_sems, out_sems, product_sems,
):
    pairs = ((q_hbm, q_ref), (g_hbm, g_ref), (ahead_hbm, ahead_ref), (w_hbm, w_ref))
    copies_in = [pltpu.make_async_copy(source, held, in_sems.at[n]) for n, (source, held) in enumerate(pairs)]
    for copy in copies_in:
        copy.start()
    tokens, width = q_ref.shape
    heads = width // HEAD_DIM
    chunk = 4 * PART
    core = units_ref[units_ref.shape[0] - 1]
    chunks = [pl.ds(c * chunk, chunk) for c in range(x.shape[0] // chunk)]
    head_cols = [pl.ds(h * HEAD_DIM, HEAD_DIM) for h in range(heads)]
    for copy in copies_in[:3]:
        copy.wait()
    for h, cols in enumerate(head_cols):
        q_rows[:, cols] = span_rows(q_ref[:, cols], ahead_ref[:, cols])
        g_rows[:, cols] = span_rows(g_ref[:, cols], ahead_ref[:, pl.ds(width + h * HEAD_DIM, HEAD_DIM)])
    copies_in[3].wait()
    for rows in chunks:
        for kind, out in enumerate((key, value)):
            out[rows, :] = dot(x[rows, :], w_ref[kind], NN).astype(jnp.bfloat16)
    for j in range(tokens // SPAN):
        starts = [pl.multiple_of(units_ref[j * 4 + r] * PART, PART) for r in range(4)]
        rows = pl.ds(j * SPAN, SPAN)
        qs = [q_rows[rows, cols] for cols in head_cols]
        gs = [g_rows[rows, cols] for cols in head_cols]
        ks = [jnp.concatenate([key[pl.ds(s, PART), cols] for s in starts], axis=0) for cols in head_cols]
        vs = [jnp.concatenate([value[pl.ds(s, PART), cols] for s in starts], axis=0) for cols in head_cols]
        scores = [dot(q, k, NT) * SCALE for q, k in zip(qs, ks)]
        d_weights = [dot(g, v, NT) for g, v in zip(gs, vs)]
        lows, d_scores = [], []
        for s, dw in zip(scores, d_weights):
            raised = jnp.exp(s - jnp.max(s, axis=-1, keepdims=True))
            weights = raised * (1.0 / jnp.sum(raised, axis=-1, keepdims=True))
            inner = jnp.sum(weights * dw, axis=-1, keepdims=True)
            lows.append(weights.astype(jnp.bfloat16))
            d_scores.append((weights * (dw - inner) * SCALE).astype(jnp.bfloat16))
        for h, cols in enumerate(head_cols):
            att[rows, cols] = dot(lows[h], vs[h], NN)
            dq[rows, cols] = dot(d_scores[h], ks[h], NN)
            dk = dot(d_scores[h], qs[h], TN).astype(jnp.bfloat16)
            dv = dot(lows[h], gs[h], TN).astype(jnp.bfloat16)
            for r, s in enumerate(starts):
                grad[0, pl.ds(s, PART), cols] = dk[r * PART : (r + 1) * PART]
                grad[1, pl.ds(s, PART), cols] = dv[r * PART : (r + 1) * PART]
    partial_copies = []
    for c, rows in enumerate(chunks):
        term = dot(grad[0, rows, :], w_ref[0], NT) + dot(grad[1, rows, :], w_ref[1], NT)
        partial[rows, :] = term.astype(jnp.bfloat16)
        copy = pltpu.make_async_copy(partial.at[rows], partial_hbm.at[rows], out_sems.at[c])
        copy.start()
        partial_copies.append(copy)
    product_copies = []
    for n in range(x.shape[1] // 128):
        e = pl.ds(n * 128, 128)
        part = x[:, n * 128 : (n + 1) * 128].T
        sent[e, :] = dot(part, grad[1 - core], NN).astype(jnp.bfloat16)
        kept[e, :] = dot(part, grad[core], NN)
        for m, (held, out) in enumerate(((sent, sent_hbm), (kept, kept_hbm))):
            copy = pltpu.make_async_copy(held.at[e], out.at[e], product_sems.at[n, m])
            copy.start()
            product_copies.append(copy)
    for cols in head_cols:
        rows_ref[0, :, cols] = pltpu.roll(att[:, cols], LEAD, 0).astype(jnp.bfloat16)
        rows_ref[1, :, cols] = pltpu.roll(dq[:, cols], LEAD, 0).astype(jnp.bfloat16)
    for copy in partial_copies + product_copies:
        copy.wait()


def low(*shape):
    return jax.ShapeDtypeStruct(shape, jnp.bfloat16)


def wide(*shape):
    return jax.ShapeDtypeStruct(shape, jnp.float32)


def call(body, name, out_shape, scratch, place, *args):
    return pl.pallas_call(
        body,
        out_shape=out_shape,
        in_specs=[SMEM] + [VMEM] * len(args),
        out_specs=jax.tree.map(lambda _: VMEM, out_shape),
        scratch_shapes=scratch,
        compiler_params=PARAMS,
        name=name,
    )(place, *args)


def block(scalars, q, g, ahead, w, x):
    tokens, width = q.shape
    all_rows, enc_width = x.shape
    rows = pltpu.VMEM((all_rows, width), jnp.bfloat16)
    half = pltpu.VMEM((tokens, width), jnp.bfloat16)
    return pl.pallas_call(
        block_body,
        out_shape=[low(2, tokens, width)]
        + [low(enc_width, width), wide(enc_width, width), low(all_rows, enc_width)],
        in_specs=[SMEM] + [HBM] * 4 + [VMEM],
        out_specs=[VMEM] + [HBM] * 3,
        scratch_shapes=[rows, rows, pltpu.VMEM((2, all_rows, width), jnp.bfloat16)]
        + [pltpu.VMEM((all_rows, enc_width), jnp.bfloat16), pltpu.VMEM((enc_width, width), jnp.bfloat16)]
        + [pltpu.VMEM((enc_width, width), jnp.float32), half, half]
        + [pltpu.VMEM(ahead.shape, jnp.bfloat16), pltpu.VMEM(w.shape, jnp.bfloat16), half, half]
        + [pltpu.VMEM((tokens, width), jnp.float32)] * 2
        + [pltpu.SemaphoreType.DMA((4,))] * 2
        + [pltpu.SemaphoreType.DMA((enc_width // 128, 2))],
        compiler_params=pltpu.CompilerParams(vmem_limit_bytes=51 * 1024 * 1024),
        name="block",
    )(scalars, q, g, ahead, w, x)


def cut(place, kept, away):
    enc_width, width = kept.shape
    rows = enc_width // 8

    def body(place_ref, kept_ref, away_ref, own_ref, *send_refs):
        x = place_ref[1]
        for high in range(2):
            for k in range(4):
                at = pl.multiple_of((high * 4 + lax.rem(x + k, 4)) * rows, 16)
                term = add(kept_ref[pl.ds(at, rows), :], away_ref[pl.ds(at, rows), :])
                if k:
                    send_refs[k - 1][high] = term.astype(jnp.bfloat16)
                else:
                    own_ref[high] = term

    return call(body, "cut", [wide(2, rows, width)] + [low(2, rows, width)] * 3, [], place, kept, away)


def spread(x, groups):
    units, piece, enc_width = x.shape
    parts = [pl.ds(c, units // 4) for c in range(0, units, units // 4)]

    def body(x_hbm, out_hbm, held, in_sems, out_sems):
        ins = [pltpu.make_async_copy(x_hbm.at[part], held.at[part], in_sems.at[c]) for c, part in enumerate(parts)]
        for copy in ins:
            copy.start()
        outs = []
        for c, part in enumerate(parts):
            ins[c].wait()
            for n in range(groups):
                copy = pltpu.make_async_copy(held.at[part], out_hbm.at[part, n], out_sems.at[c, n])
                copy.start()
                outs.append(copy)
        for copy in outs:
            copy.wait()

    return pl.pallas_call(
        body,
        out_shape=low(units, groups, piece, enc_width),
        in_specs=[HBM],
        out_specs=HBM,
        scratch_shapes=[
            pltpu.VMEM(x.shape, jnp.bfloat16),
            pltpu.SemaphoreType.DMA((4,)),
            pltpu.SemaphoreType.DMA((4, groups)),
        ],
        compiler_params=pltpu.CompilerParams(vmem_limit_bytes=56 * 1024 * 1024),
        name="spread",
    )(x)


def gather_up(place, terms, done, behind):
    units, groups, piece, enc_width = terms.shape
    _, tokens, width = done.shape

    def body(_, terms_ref, done_ref, behind_ref, total_ref, att_ref, dq_ref, token_ref):
        token_ref[...] = jnp.zeros(token_ref.shape, jnp.float32)
        for u in range(units):
            total = add(terms_ref[u, 0], terms_ref[u, 1])
            for n in range(2, groups):
                total = add(total, terms_ref[u, n])
            total_ref[u] = total.astype(jnp.bfloat16)
        lead = lax.broadcasted_iota(jnp.int32, (SPAN, width), 0) < LEAD
        for n, full in enumerate((att_ref, dq_ref)):
            came, own = behind_ref[n].astype(jnp.float32), done_ref[n, :SPAN, :].astype(jnp.float32)
            full[:SPAN, :] = jnp.where(lead, came, own).astype(jnp.bfloat16)
            full[SPAN:, :] = done_ref[n, SPAN:, :]

    out_shape = [low(units, piece, enc_width), low(tokens, width), low(tokens, width), wide(8, 128)]
    return call(body, "gather_up", out_shape, [], place, terms, done, behind)


def sum_rows(place, name, rows, *after):
    def body(_, *refs):
        terms = [ref[...] for ref in refs[: len(rows)]]
        while len(terms) > 1:
            terms = [add(a, b) for a, b in zip(terms[::2], terms[1::2])]
        refs[-1][...] = terms[0].astype(jnp.bfloat16)

    return pl.pallas_call(
        body,
        out_shape=low(*rows[0].shape),
        in_specs=[SMEM] + [VMEM] * (len(rows) + len(after)),
        out_specs=VMEM,
        compiler_params=PARAMS,
        name=name,
    )(place, *rows, *after)


def permute(x, axis, to):
    n = lax.axis_size(axis)
    return lax.ppermute(x, axis, [(i, to(i)) for i in range(n) if 0 <= to(i) < n])


def exchange(x):
    outer, inner, *rest = x.shape
    x = lax.all_to_all(x.reshape(outer * inner, *rest), ("ctx", "nbr"), split_axis=0, concat_axis=0, tiled=True)
    return x.reshape(outer, inner, *rest)


def shards(queries, cotangent, encoded, kv_weight, neighbour_ids):
    q, g, enc = queries[0], cotangent[0], encoded[0]
    units, piece, enc_width = enc.shape
    groups = lax.axis_size("nbr")
    ctx = lax.axis_index("ctx")
    dp = lax.axis_index("dp")
    place = jnp.stack((ctx % 2, dp % 4, dp // 4)).astype(jnp.int32)

    x = exchange(spread(enc, groups)).reshape(units * PART, enc_width)

    head = jnp.concatenate((q[:SPAN], g[:SPAN]), axis=1)
    ahead = permute(head, "ctx", lambda i: i - 1)

    unit_of = (neighbour_ids[0] // units).reshape(-1)
    scalars = jnp.concatenate((unit_of, (ctx % 2)[None])).astype(jnp.int32)
    done, sent, kept, partial = block(scalars, q, g, ahead, kv_weight, x)

    terms = exchange(partial.reshape(units, groups, piece, enc_width))
    behind = permute(done[:, :SPAN], "ctx", lambda i: i + 1)

    held, *sends = cut(place, kept, permute(sent, "ctx", lambda i: i ^ 1))
    for k in (1, 3, 2):
        held = add(held, permute(sends[k - 1], "dp", lambda i, k=k: i // 4 * 4 + (i + k) % 4))
    high = dp // 4
    held = held.astype(jnp.bfloat16)
    other = lax.dynamic_index_in_dim(held, 1 - high, 0, keepdims=False)
    mine = lax.dynamic_index_in_dim(held, high, 0, keepdims=False)
    owners = lax.axis_size("ctx")
    quad = (
        mine,
        permute(other, "dp", lambda i: i ^ 4),
        permute(mine, "ctx", lambda i: i ^ 2),
        permute(other, ("dp", "ctx"), lambda i: i ^ (4 * owners + 2)),
    )
    rows = sum_rows(place, "z_and_y", quad, behind)
    encoded_grad, attended, query_grad, token = gather_up(place, terms, done, behind)
    rows = sum_rows(place, "y", (rows, permute(rows, "ctx", lambda i: i ^ 4)), token)
    mine = add(rows, permute(rows, "ctx", lambda i: i ^ 8))
    theirs = permute(mine, "ctx", lambda i: i ^ 1)
    keys_here = ctx % 2 == 0
    weight_grad = jnp.stack((jnp.where(keys_here, mine, theirs), jnp.where(keys_here, theirs, mine)), axis=0)
    return (attended[None], query_grad[None], encoded_grad[None], weight_grad)


def add(a, b):
    return a.astype(jnp.float32) + b.astype(jnp.float32)


def solution(mesh):
    return jax.shard_map(
        shards,
        mesh=mesh,
        in_specs=(
            P("dp", "ctx", "nbr"),
            P("dp", "ctx", "nbr"),
            P("dp", "ctx", "nbr", None),
            P(None, None, "nbr"),
            P("dp", "ctx", None),
        ),
        out_specs=(
            P("dp", "ctx", "nbr"),
            P("dp", "ctx", "nbr"),
            P("dp", "ctx", "nbr", None),
            P(None, "dp", "nbr"),
        ),
        check_vma=False,
    )
```

```python
import math

import jax
import jax.numpy as jnp
from jax import lax
from jax.experimental import pallas as pl
from jax.experimental.pallas import tpu as pltpu
from jax.sharding import PartitionSpec as P

HEAD_DIM = 128
SPAN = 64
PART = 64
LEAD = SPAN - 1
SCALE = 1.0 / math.sqrt(HEAD_DIM)
NT = (((1,), (1,)), ((), ()))
TN = (((0,), (0,)), ((), ()))
NN = (((1,), (0,)), ((), ()))
VMEM = pl.BlockSpec(memory_space=pltpu.VMEM)
SMEM = pl.BlockSpec(memory_space=pltpu.SMEM)
HBM = pl.BlockSpec(memory_space=pltpu.HBM)
PARAMS = pltpu.CompilerParams(vmem_limit_bytes=50 * 1024 * 1024)


def dot(a, b, dims):
    return lax.dot_general(a, b, dims, preferred_element_type=jnp.float32)


def span_rows(own, ahead):
    own, ahead = own.astype(jnp.float32), ahead.astype(jnp.float32)
    row = lax.broadcasted_iota(jnp.int32, ahead.shape, 0)
    mixed = jnp.concatenate((jnp.where(row < LEAD, ahead, own[:SPAN]), own[SPAN:]), axis=0)
    return pltpu.roll(mixed, own.shape[0] - LEAD, 0).astype(jnp.bfloat16)


def block_body(
    units_ref, q_hbm, g_hbm, ahead_hbm, w_hbm, x, rows_ref, sent_hbm, kept_hbm, partial_hbm,
    key, value, grad, partial, sent, kept, q_ref, g_ref, ahead_ref, w_ref, q_rows, g_rows, att, dq, in_sems, out_sems, product_sems,
):
    pairs = ((w_hbm.at[0], w_ref.at[0]), (w_hbm.at[1], w_ref.at[1]), (q_hbm, q_ref), (g_hbm, g_ref), (ahead_hbm, ahead_ref))
    copies_in = [pltpu.make_async_copy(source, held, in_sems.at[n]) for n, (source, held) in enumerate(pairs)]
    for copy in copies_in:
        copy.start()
    tokens, width = q_ref.shape
    heads = width // HEAD_DIM
    chunk = 4 * PART
    core = units_ref[units_ref.shape[0] - 1]
    chunks = [pl.ds(c * chunk, chunk) for c in range(x.shape[0] // chunk)]
    head_cols = [pl.ds(h * HEAD_DIM, HEAD_DIM) for h in range(heads)]
    for kind, out in enumerate((key, value)):
        copies_in[kind].wait()
        for rows in chunks:
            out[rows, :] = dot(x[rows, :], w_ref[kind], NN).astype(jnp.bfloat16)
    for copy in copies_in[2:]:
        copy.wait()
    for h, cols in enumerate(head_cols):
        q_rows[:, cols] = span_rows(q_ref[:, cols], ahead_ref[:, cols])
        g_rows[:, cols] = span_rows(g_ref[:, cols], ahead_ref[:, pl.ds(width + h * HEAD_DIM, HEAD_DIM)])
    for j in range(tokens // SPAN):
        starts = [pl.multiple_of(units_ref[j * 4 + r] * PART, PART) for r in range(4)]
        rows = pl.ds(j * SPAN, SPAN)
        qs = [q_rows[rows, cols] for cols in head_cols]
        gs = [g_rows[rows, cols] for cols in head_cols]
        ks = [jnp.concatenate([key[pl.ds(s, PART), cols] for s in starts], axis=0) for cols in head_cols]
        vs = [jnp.concatenate([value[pl.ds(s, PART), cols] for s in starts], axis=0) for cols in head_cols]
        scores = [dot(q, k, NT) * SCALE for q, k in zip(qs, ks)]
        d_weights = [dot(g, v, NT) for g, v in zip(gs, vs)]
        lows, d_scores = [], []
        for s, dw in zip(scores, d_weights):
            raised = jnp.exp(s - jnp.max(s, axis=-1, keepdims=True))
            weights = raised * (1.0 / jnp.sum(raised, axis=-1, keepdims=True))
            inner = jnp.sum(weights * dw, axis=-1, keepdims=True)
            lows.append(weights.astype(jnp.bfloat16))
            d_scores.append((weights * (dw - inner) * SCALE).astype(jnp.bfloat16))
        for h, cols in enumerate(head_cols):
            att[rows, cols] = dot(lows[h], vs[h], NN)
            dq[rows, cols] = dot(d_scores[h], ks[h], NN)
            dk = dot(d_scores[h], qs[h], TN).astype(jnp.bfloat16)
            dv = dot(lows[h], gs[h], TN).astype(jnp.bfloat16)
            for r, s in enumerate(starts):
                grad[0, pl.ds(s, PART), cols] = dk[r * PART : (r + 1) * PART]
                grad[1, pl.ds(s, PART), cols] = dv[r * PART : (r + 1) * PART]
    partial_copies = []
    for c, rows in enumerate(chunks):
        term = dot(grad[0, rows, :], w_ref[0], NT) + dot(grad[1, rows, :], w_ref[1], NT)
        partial[rows, :] = term.astype(jnp.bfloat16)
        copy = pltpu.make_async_copy(partial.at[rows], partial_hbm.at[rows], out_sems.at[c])
        copy.start()
        partial_copies.append(copy)
    product_copies = []
    for n in range(x.shape[1] // 128):
        e = pl.ds(n * 128, 128)
        part = x[:, n * 128 : (n + 1) * 128].T
        sent[e, :] = dot(part, grad[1 - core], NN).astype(jnp.bfloat16)
        kept[e, :] = dot(part, grad[core], NN)
        for m, (held, out) in enumerate(((sent, sent_hbm), (kept, kept_hbm))):
            copy = pltpu.make_async_copy(held.at[e], out.at[e], product_sems.at[n, m])
            copy.start()
            product_copies.append(copy)
    for cols in head_cols:
        rows_ref[0, :, cols] = pltpu.roll(att[:, cols], LEAD, 0).astype(jnp.bfloat16)
        rows_ref[1, :, cols] = pltpu.roll(dq[:, cols], LEAD, 0).astype(jnp.bfloat16)
    for copy in partial_copies + product_copies:
        copy.wait()


def low(*shape):
    return jax.ShapeDtypeStruct(shape, jnp.bfloat16)


def wide(*shape):
    return jax.ShapeDtypeStruct(shape, jnp.float32)


def call(body, name, out_shape, scratch, place, *args):
    return pl.pallas_call(
        body,
        out_shape=out_shape,
        in_specs=[SMEM] + [VMEM] * len(args),
        out_specs=jax.tree.map(lambda _: VMEM, out_shape),
        scratch_shapes=scratch,
        compiler_params=PARAMS,
        name=name,
    )(place, *args)


def block(scalars, q, g, ahead, w, x):
    tokens, width = q.shape
    all_rows, enc_width = x.shape
    rows = pltpu.VMEM((all_rows, width), jnp.bfloat16)
    half = pltpu.VMEM((tokens, width), jnp.bfloat16)
    return pl.pallas_call(
        block_body,
        out_shape=[low(2, tokens, width)]
        + [low(enc_width, width), wide(enc_width, width), low(all_rows, enc_width)],
        in_specs=[SMEM] + [HBM] * 4 + [VMEM],
        out_specs=[VMEM] + [HBM] * 3,
        scratch_shapes=[rows, rows, pltpu.VMEM((2, all_rows, width), jnp.bfloat16)]
        + [pltpu.VMEM((all_rows, enc_width), jnp.bfloat16), pltpu.VMEM((enc_width, width), jnp.bfloat16)]
        + [pltpu.VMEM((enc_width, width), jnp.float32), half, half]
        + [pltpu.VMEM(ahead.shape, jnp.bfloat16), pltpu.VMEM(w.shape, jnp.bfloat16), half, half]
        + [pltpu.VMEM((tokens, width), jnp.float32)] * 2
        + [pltpu.SemaphoreType.DMA((5,)), pltpu.SemaphoreType.DMA((4,))]
        + [pltpu.SemaphoreType.DMA((enc_width // 128, 2))],
        compiler_params=pltpu.CompilerParams(vmem_limit_bytes=51 * 1024 * 1024),
        name="block",
    )(scalars, q, g, ahead, w, x)


def cut(place, kept, away):
    enc_width, width = kept.shape
    rows = enc_width // 8

    def body(place_ref, kept_ref, away_ref, own_ref, *send_refs):
        x = place_ref[1]
        for high in range(2):
            for k in range(4):
                at = pl.multiple_of((high * 4 + lax.rem(x + k, 4)) * rows, 16)
                term = add(kept_ref[pl.ds(at, rows), :], away_ref[pl.ds(at, rows), :])
                if k:
                    send_refs[k - 1][high] = term.astype(jnp.bfloat16)
                else:
                    own_ref[high] = term

    return call(body, "cut", [wide(2, rows, width)] + [low(2, rows, width)] * 3, [], place, kept, away)


def spread(x, groups):
    units, piece, enc_width = x.shape
    parts = [pl.ds(c, units // 4) for c in range(0, units, units // 4)]

    def body(x_hbm, out_hbm, held, in_sems, out_sems):
        ins = [pltpu.make_async_copy(x_hbm.at[part], held.at[part], in_sems.at[c]) for c, part in enumerate(parts)]
        for copy in ins:
            copy.start()
        outs = []
        for c, part in enumerate(parts):
            ins[c].wait()
            for n in range(groups):
                copy = pltpu.make_async_copy(held.at[part], out_hbm.at[part, n], out_sems.at[c, n])
                copy.start()
                outs.append(copy)
        for copy in outs:
            copy.wait()

    return pl.pallas_call(
        body,
        out_shape=low(units, groups, piece, enc_width),
        in_specs=[HBM],
        out_specs=HBM,
        scratch_shapes=[
            pltpu.VMEM(x.shape, jnp.bfloat16),
            pltpu.SemaphoreType.DMA((4,)),
            pltpu.SemaphoreType.DMA((4, groups)),
        ],
        compiler_params=pltpu.CompilerParams(vmem_limit_bytes=56 * 1024 * 1024),
        name="spread",
    )(x)


def gather_up(place, terms, done, behind):
    units, groups, piece, enc_width = terms.shape
    _, tokens, width = done.shape

    def body(_, terms_ref, done_ref, behind_ref, total_ref, att_ref, dq_ref, token_ref):
        token_ref[...] = jnp.zeros(token_ref.shape, jnp.float32)
        for u in range(units):
            total = add(terms_ref[u, 0], terms_ref[u, 1])
            for n in range(2, groups):
                total = add(total, terms_ref[u, n])
            total_ref[u] = total.astype(jnp.bfloat16)
        lead = lax.broadcasted_iota(jnp.int32, (SPAN, width), 0) < LEAD
        for n, full in enumerate((att_ref, dq_ref)):
            came, own = behind_ref[n].astype(jnp.float32), done_ref[n, :SPAN, :].astype(jnp.float32)
            full[:SPAN, :] = jnp.where(lead, came, own).astype(jnp.bfloat16)
            full[SPAN:, :] = done_ref[n, SPAN:, :]

    out_shape = [low(units, piece, enc_width), low(tokens, width), low(tokens, width), wide(8, 128)]
    return call(body, "gather_up", out_shape, [], place, terms, done, behind)


def sum_rows(place, name, rows, *after):
    def body(_, *refs):
        terms = [ref[...] for ref in refs[: len(rows)]]
        while len(terms) > 1:
            terms = [add(a, b) for a, b in zip(terms[::2], terms[1::2])]
        refs[-1][...] = terms[0].astype(jnp.bfloat16)

    return pl.pallas_call(
        body,
        out_shape=low(*rows[0].shape),
        in_specs=[SMEM] + [VMEM] * (len(rows) + len(after)),
        out_specs=VMEM,
        compiler_params=PARAMS,
        name=name,
    )(place, *rows, *after)


def permute(x, axis, to):
    n = lax.axis_size(axis)
    return lax.ppermute(x, axis, [(i, to(i)) for i in range(n) if 0 <= to(i) < n])


def exchange(x):
    outer, inner, *rest = x.shape
    x = lax.all_to_all(x.reshape(outer * inner, *rest), ("ctx", "nbr"), split_axis=0, concat_axis=0, tiled=True)
    return x.reshape(outer, inner, *rest)


def shards(queries, cotangent, encoded, kv_weight, neighbour_ids):
    q, g, enc = queries[0], cotangent[0], encoded[0]
    units, piece, enc_width = enc.shape
    groups = lax.axis_size("nbr")
    ctx = lax.axis_index("ctx")
    dp = lax.axis_index("dp")
    place = jnp.stack((ctx % 2, dp % 4, dp // 4)).astype(jnp.int32)

    x = exchange(spread(enc, groups)).reshape(units * PART, enc_width)

    head = jnp.concatenate((q[:SPAN], g[:SPAN]), axis=1)
    ahead = permute(head, "ctx", lambda i: i - 1)

    unit_of = (neighbour_ids[0] // units).reshape(-1)
    scalars = jnp.concatenate((unit_of, (ctx % 2)[None])).astype(jnp.int32)
    done, sent, kept, partial = block(scalars, q, g, ahead, kv_weight, x)

    terms = exchange(partial.reshape(units, groups, piece, enc_width))
    behind = permute(done[:, :SPAN], "ctx", lambda i: i + 1)

    held, *sends = cut(place, kept, permute(sent, "ctx", lambda i: i ^ 1))
    for k in (1, 3, 2):
        held = add(held, permute(sends[k - 1], "dp", lambda i, k=k: i // 4 * 4 + (i + k) % 4))
    high = dp // 4
    held = held.astype(jnp.bfloat16)
    other = lax.dynamic_index_in_dim(held, 1 - high, 0, keepdims=False)
    mine = lax.dynamic_index_in_dim(held, high, 0, keepdims=False)
    owners = lax.axis_size("ctx")
    quad = (
        mine,
        permute(other, "dp", lambda i: i ^ 4),
        permute(mine, "ctx", lambda i: i ^ 2),
        permute(other, ("dp", "ctx"), lambda i: i ^ (4 * owners + 2)),
    )
    rows = sum_rows(place, "z_and_y", quad, behind)
    encoded_grad, attended, query_grad, token = gather_up(place, terms, done, behind)
    rows = sum_rows(place, "y", (rows, permute(rows, "ctx", lambda i: i ^ 4)), token)
    mine = add(rows, permute(rows, "ctx", lambda i: i ^ 8))
    theirs = permute(mine, "ctx", lambda i: i ^ 1)
    keys_here = ctx % 2 == 0
    weight_grad = jnp.stack((jnp.where(keys_here, mine, theirs), jnp.where(keys_here, theirs, mine)), axis=0)
    return (attended[None], query_grad[None], encoded_grad[None], weight_grad)


def add(a, b):
    return a.astype(jnp.float32) + b.astype(jnp.float32)


def solution(mesh):
    return jax.shard_map(
        shards,
        mesh=mesh,
        in_specs=(
            P("dp", "ctx", "nbr"),
            P("dp", "ctx", "nbr"),
            P("dp", "ctx", "nbr", None),
            P(None, None, "nbr"),
            P("dp", "ctx", None),
        ),
        out_specs=(
            P("dp", "ctx", "nbr"),
            P("dp", "ctx", "nbr"),
            P("dp", "ctx", "nbr", None),
            P(None, "dp", "nbr"),
        ),
        check_vma=False,
    )
```

```python
import math

import jax
import jax.numpy as jnp
from jax import lax
from jax.experimental import pallas as pl
from jax.experimental.pallas import tpu as pltpu
from jax.sharding import PartitionSpec as P

HEAD_DIM = 128
SPAN = 64
PART = 64
LEAD = SPAN - 1
SCALE = 1.0 / math.sqrt(HEAD_DIM)
NT = (((1,), (1,)), ((), ()))
TN = (((0,), (0,)), ((), ()))
NN = (((1,), (0,)), ((), ()))
VMEM = pl.BlockSpec(memory_space=pltpu.VMEM)
SMEM = pl.BlockSpec(memory_space=pltpu.SMEM)
HBM = pl.BlockSpec(memory_space=pltpu.HBM)
PARAMS = pltpu.CompilerParams(vmem_limit_bytes=50 * 1024 * 1024)


def dot(a, b, dims):
    return lax.dot_general(a, b, dims, preferred_element_type=jnp.float32)


def span_rows(own, ahead):
    own, ahead = own.astype(jnp.float32), ahead.astype(jnp.float32)
    row = lax.broadcasted_iota(jnp.int32, ahead.shape, 0)
    mixed = jnp.concatenate((jnp.where(row < LEAD, ahead, own[:SPAN]), own[SPAN:]), axis=0)
    return pltpu.roll(mixed, own.shape[0] - LEAD, 0).astype(jnp.bfloat16)


def block_body(
    units_ref, q_hbm, g_hbm, ahead_hbm, w_hbm, x, att_ref, dq_ref, tail_ref, sent_ref, kept_ref, partial_hbm,
    key, value, grad, partial, q_ref, g_ref, ahead_ref, w_ref, q_rows, g_rows, att, dq, in_sems, out_sems,
):
    pairs = ((w_hbm, w_ref), (q_hbm, q_ref), (g_hbm, g_ref), (ahead_hbm, ahead_ref))
    copies_in = [pltpu.make_async_copy(source, held, in_sems.at[n]) for n, (source, held) in enumerate(pairs)]
    for copy in copies_in:
        copy.start()
    tokens, width = q_ref.shape
    heads = width // HEAD_DIM
    chunk = 4 * PART
    core = units_ref[units_ref.shape[0] - 1]
    chunks = [pl.ds(c * chunk, chunk) for c in range(x.shape[0] // chunk)]
    head_cols = [pl.ds(h * HEAD_DIM, HEAD_DIM) for h in range(heads)]
    copies_in[0].wait()
    for rows in chunks:
        for kind, out in enumerate((key, value)):
            out[rows, :] = dot(x[rows, :], w_ref[kind], NN).astype(jnp.bfloat16)
    for copy in copies_in[1:]:
        copy.wait()
    for h, cols in enumerate(head_cols):
        q_rows[:, cols] = span_rows(q_ref[:, cols], ahead_ref[:, cols])
        g_rows[:, cols] = span_rows(g_ref[:, cols], ahead_ref[:, pl.ds(width + h * HEAD_DIM, HEAD_DIM)])
    for j in range(tokens // SPAN):
        starts = [pl.multiple_of(units_ref[j * 4 + r] * PART, PART) for r in range(4)]
        rows = pl.ds(j * SPAN, SPAN)
        qs = [q_rows[rows, cols] for cols in head_cols]
        gs = [g_rows[rows, cols] for cols in head_cols]
        ks = [jnp.concatenate([key[pl.ds(s, PART), cols] for s in starts], axis=0) for cols in head_cols]
        vs = [jnp.concatenate([value[pl.ds(s, PART), cols] for s in starts], axis=0) for cols in head_cols]
        scores = [dot(q, k, NT) * SCALE for q, k in zip(qs, ks)]
        d_weights = [dot(g, v, NT) for g, v in zip(gs, vs)]
        lows, d_scores = [], []
        for s, dw in zip(scores, d_weights):
            raised = jnp.exp(s - jnp.max(s, axis=-1, keepdims=True))
            weights = raised * (1.0 / jnp.sum(raised, axis=-1, keepdims=True))
            inner = jnp.sum(weights * dw, axis=-1, keepdims=True)
            lows.append(weights.astype(jnp.bfloat16))
            d_scores.append((weights * (dw - inner) * SCALE).astype(jnp.bfloat16))
        for h, cols in enumerate(head_cols):
            att[rows, cols] = dot(lows[h], vs[h], NN)
            dq[rows, cols] = dot(d_scores[h], ks[h], NN)
            dk = dot(d_scores[h], qs[h], TN).astype(jnp.bfloat16)
            dv = dot(lows[h], gs[h], TN).astype(jnp.bfloat16)
            for r, s in enumerate(starts):
                grad[0, pl.ds(s, PART), cols] = dk[r * PART : (r + 1) * PART]
                grad[1, pl.ds(s, PART), cols] = dv[r * PART : (r + 1) * PART]
    partial_copies = []
    for c, rows in enumerate(chunks):
        term = dot(grad[0, rows, :], w_ref[0], NT) + dot(grad[1, rows, :], w_ref[1], NT)
        partial[rows, :] = term.astype(jnp.bfloat16)
        copy = pltpu.make_async_copy(partial.at[rows], partial_hbm.at[rows], out_sems.at[c])
        copy.start()
        partial_copies.append(copy)
    for e in range(0, x.shape[1], 128):
        part = x[:, e : e + 128].T
        sent_ref[e : e + 128, :] = dot(part, grad[1 - core], NN).astype(jnp.bfloat16)
        kept_ref[e : e + 128, :] = dot(part, grad[core], NN)
    for cols in head_cols:
        att_ref[:, cols] = pltpu.roll(att[:, cols], LEAD, 0).astype(jnp.bfloat16)
        dq_ref[:, cols] = pltpu.roll(dq[:, cols], LEAD, 0).astype(jnp.bfloat16)
    tail_ref[:, :width] = att_ref[:SPAN, :]
    tail_ref[:, width:] = dq_ref[:SPAN, :]
    for copy in partial_copies:
        copy.wait()


def low(*shape):
    return jax.ShapeDtypeStruct(shape, jnp.bfloat16)


def wide(*shape):
    return jax.ShapeDtypeStruct(shape, jnp.float32)


def call(body, name, out_shape, scratch, place, *args):
    return pl.pallas_call(
        body,
        out_shape=out_shape,
        in_specs=[SMEM] + [VMEM] * len(args),
        out_specs=jax.tree.map(lambda _: VMEM, out_shape),
        scratch_shapes=scratch,
        compiler_params=PARAMS,
        name=name,
    )(place, *args)


def block(scalars, q, g, ahead, w, x):
    tokens, width = q.shape
    all_rows, enc_width = x.shape
    rows = pltpu.VMEM((all_rows, width), jnp.bfloat16)
    half = pltpu.VMEM((tokens, width), jnp.bfloat16)
    return pl.pallas_call(
        block_body,
        out_shape=[low(tokens, width), low(tokens, width), low(SPAN, 2 * width)]
        + [low(enc_width, width), wide(enc_width, width), low(all_rows, enc_width)],
        in_specs=[SMEM] + [HBM] * 4 + [VMEM],
        out_specs=[VMEM] * 5 + [HBM],
        scratch_shapes=[rows, rows, pltpu.VMEM((2, all_rows, width), jnp.bfloat16)]
        + [pltpu.VMEM((all_rows, enc_width), jnp.bfloat16), half, half]
        + [pltpu.VMEM(ahead.shape, jnp.bfloat16), pltpu.VMEM(w.shape, jnp.bfloat16), half, half]
        + [pltpu.VMEM((tokens, width), jnp.float32)] * 2
        + [pltpu.SemaphoreType.DMA((4,))] * 2,
        compiler_params=pltpu.CompilerParams(vmem_limit_bytes=52 * 1024 * 1024),
        name="block",
    )(scalars, q, g, ahead, w, x)


def cut(place, kept, away):
    enc_width, width = kept.shape
    rows = enc_width // 8

    def body(place_ref, kept_ref, away_ref, own_ref, *send_refs):
        x = place_ref[1]
        for high in range(2):
            for k in range(4):
                at = pl.multiple_of((high * 4 + lax.rem(x + k, 4)) * rows, 16)
                term = add(kept_ref[pl.ds(at, rows), :], away_ref[pl.ds(at, rows), :])
                if k:
                    send_refs[k - 1][high] = term.astype(jnp.bfloat16)
                else:
                    own_ref[high] = term

    return call(body, "cut", [wide(2, rows, width)] + [low(2, rows, width)] * 3, [], place, kept, away)


def spread(x, groups):
    units, piece, enc_width = x.shape
    parts = [pl.ds(c, units // 4) for c in range(0, units, units // 4)]

    def body(x_hbm, out_hbm, held, in_sems, out_sems):
        ins = [pltpu.make_async_copy(x_hbm.at[part], held.at[part], in_sems.at[c]) for c, part in enumerate(parts)]
        for copy in ins:
            copy.start()
        outs = []
        for c, part in enumerate(parts):
            ins[c].wait()
            for n in range(groups):
                copy = pltpu.make_async_copy(held.at[part], out_hbm.at[part, n], out_sems.at[c, n])
                copy.start()
                outs.append(copy)
        for copy in outs:
            copy.wait()

    return pl.pallas_call(
        body,
        out_shape=low(units, groups, piece, enc_width),
        in_specs=[HBM],
        out_specs=HBM,
        scratch_shapes=[
            pltpu.VMEM(x.shape, jnp.bfloat16),
            pltpu.SemaphoreType.DMA((4,)),
            pltpu.SemaphoreType.DMA((4, groups)),
        ],
        compiler_params=pltpu.CompilerParams(vmem_limit_bytes=56 * 1024 * 1024),
        name="spread",
    )(x)


def gather_up(place, terms, att, dq, behind):
    units, groups, piece, enc_width = terms.shape
    width = att.shape[1]

    def body(_, terms_ref, att_ref, dq_ref, behind_ref, total_ref, *refs):
        full_refs, token_ref = refs[:2], refs[2]
        token_ref[...] = jnp.zeros(token_ref.shape, jnp.float32)
        for u in range(units):
            total = add(terms_ref[u, 0], terms_ref[u, 1])
            for n in range(2, groups):
                total = add(total, terms_ref[u, n])
            total_ref[u] = total.astype(jnp.bfloat16)
        lead = lax.broadcasted_iota(jnp.int32, (SPAN, width), 0) < LEAD
        for n, (ref, full) in enumerate(zip((att_ref, dq_ref), full_refs)):
            came = behind_ref[:, n * width : (n + 1) * width].astype(jnp.float32)
            full[:SPAN, :] = jnp.where(lead, came, ref[:SPAN, :].astype(jnp.float32)).astype(jnp.bfloat16)
            full[SPAN:, :] = ref[SPAN:, :]

    out_shape = [low(units, piece, enc_width), low(*att.shape), low(*dq.shape), wide(8, 128)]
    return call(body, "gather_up", out_shape, [], place, terms, att, dq, behind)


def sum_rows(place, name, rows, *after):
    def body(_, *refs):
        terms = [ref[...] for ref in refs[: len(rows)]]
        while len(terms) > 1:
            terms = [add(a, b) for a, b in zip(terms[::2], terms[1::2])]
        refs[-1][...] = terms[0].astype(jnp.bfloat16)

    return pl.pallas_call(
        body,
        out_shape=low(*rows[0].shape),
        in_specs=[SMEM] + [VMEM] * (len(rows) + len(after)),
        out_specs=VMEM,
        compiler_params=PARAMS,
        name=name,
    )(place, *rows, *after)


def permute(x, axis, to):
    n = lax.axis_size(axis)
    return lax.ppermute(x, axis, [(i, to(i)) for i in range(n) if 0 <= to(i) < n])


def exchange(x):
    outer, inner, *rest = x.shape
    x = lax.all_to_all(x.reshape(outer * inner, *rest), ("ctx", "nbr"), split_axis=0, concat_axis=0, tiled=True)
    return x.reshape(outer, inner, *rest)


def shards(queries, cotangent, encoded, kv_weight, neighbour_ids):
    q, g, enc = queries[0], cotangent[0], encoded[0]
    units, piece, enc_width = enc.shape
    groups = lax.axis_size("nbr")
    ctx = lax.axis_index("ctx")
    dp = lax.axis_index("dp")
    place = jnp.stack((ctx % 2, dp % 4, dp // 4)).astype(jnp.int32)

    x = exchange(spread(enc, groups)).reshape(units * PART, enc_width)

    head = jnp.concatenate((q[:SPAN], g[:SPAN]), axis=1)
    ahead = permute(head, "ctx", lambda i: i - 1)

    unit_of = (neighbour_ids[0] // units).reshape(-1)
    scalars = jnp.concatenate((unit_of, (ctx % 2)[None])).astype(jnp.int32)
    att, dq, tail, sent, kept, partial = block(scalars, q, g, ahead, kv_weight, x)

    terms = exchange(partial.reshape(units, groups, piece, enc_width))
    behind = permute(tail, "ctx", lambda i: i + 1)

    held, *sends = cut(place, kept, permute(sent, "ctx", lambda i: i ^ 1))
    for k in (1, 3, 2):
        held = add(held, permute(sends[k - 1], "dp", lambda i, k=k: i // 4 * 4 + (i + k) % 4))
    high = dp // 4
    held = held.astype(jnp.bfloat16)
    other = lax.dynamic_index_in_dim(held, 1 - high, 0, keepdims=False)
    mine = lax.dynamic_index_in_dim(held, high, 0, keepdims=False)
    owners = lax.axis_size("ctx")
    quad = (
        mine,
        permute(other, "dp", lambda i: i ^ 4),
        permute(mine, "ctx", lambda i: i ^ 2),
        permute(other, ("dp", "ctx"), lambda i: i ^ (4 * owners + 2)),
    )
    rows = sum_rows(place, "z_and_y", quad, behind)
    encoded_grad, attended, query_grad, token = gather_up(place, terms, att, dq, behind)
    rows = sum_rows(place, "y", (rows, permute(rows, "ctx", lambda i: i ^ 4)), token)
    mine = add(rows, permute(rows, "ctx", lambda i: i ^ 8))
    theirs = permute(mine, "ctx", lambda i: i ^ 1)
    keys_here = ctx % 2 == 0
    weight_grad = jnp.stack((jnp.where(keys_here, mine, theirs), jnp.where(keys_here, theirs, mine)), axis=0)
    return (attended[None], query_grad[None], encoded_grad[None], weight_grad)


def add(a, b):
    return a.astype(jnp.float32) + b.astype(jnp.float32)


def solution(mesh):
    return jax.shard_map(
        shards,
        mesh=mesh,
        in_specs=(
            P("dp", "ctx", "nbr"),
            P("dp", "ctx", "nbr"),
            P("dp", "ctx", "nbr", None),
            P(None, None, "nbr"),
            P("dp", "ctx", None),
        ),
        out_specs=(
            P("dp", "ctx", "nbr"),
            P("dp", "ctx", "nbr"),
            P("dp", "ctx", "nbr", None),
            P(None, "dp", "nbr"),
        ),
        check_vma=False,
    )
```
